256 devices in a mesh: dp: 4 (over x), seq: 16 (over z_hi, y, core), head: 4 (over z_lo).
Axes of the slice: x: 4, y: 4, z: 8 (z_hi: 2, z_lo: 4; z = z_hi * 4 + z_lo), core: 2. Of those that a mesh axis runs over, the one named last changes fastest.
Arguments:
- map_thirteen: bfloat16 [32, 16, 13, 1920], P('dp', 'seq'), may hold values from -6 to 6
- kv_cache: bfloat16 [32, 256, 2, 1024], P('dp', 'seq', None, 'head'), may hold values from -6 to 6
- class_labels: int32 [32], P('dp'), may hold values from 0 to 999
- class_table: bfloat16 [1000, 3, 1920], P('head'), may hold values from -4 to 4
- sampled_ids: int32 [32, 13, 13], P('dp'), may hold values from 0 to 4095
- codebook: float32 [4096, 32], replicated, may hold values from -6 to 6
- feature_sum: float32 [32, 16, 512], P('dp', 'seq'), may hold values from -6 to 6
- embed_weight: float32 [32, 1920], replicated, may hold values from -1 to 1
- embed_bias: float32 [1920], replicated, may hold values from -3 to 3
- position_table: bfloat16 [16, 16, 1920], P('seq'), may hold values from -3 to 3
- qkv_weight: bfloat16 [1920, 3, 1024], P(None, None, 'head'), may hold values from -0.125 to 0.125
- out_weight: bfloat16 [1024, 1920], P('head'), may hold values from -0.1875 to 0.1875
- head_scale: float32 [16], P('head'), may hold values from 2 to 40
Outputs:
- branch_thirteen: bfloat16 [32, 16, 13, 1920], P('dp', 'seq')
- branch_sixteen: bfloat16 [32, 16, 16, 1920], P('dp', 'seq')
The draws below stay inside these ranges and needn't reach their ends.
All inputs are finite; a program needn't handle non-finite values.
Results may differ from the reference program's by a relative error of at most 0.011.
Values may be sent and summed in bfloat16 or wider, within the bound.
A program may use at most 64 MiB of HBM per device.

```python
import math
import jax
import jax.numpy as jnp
import numpy as np
from jax import lax

D = 1920
HDIM = 64
HEADS = 16
CLASSES = 1000
VOCAB = 4096
CDIM = 32
S13 = 13
S16 = 16
COARSE = 255
CACHE = 256
IMGS = 32


def touch_ends(result, own_key, smallest, high):
    longest = result.shape.index(max(result.shape))
    spots = []
    for shift in (0, 1):
        where = [jax.random.randint(jax.random.fold_in(own_key, axis), (), 0, length) for axis, length in enumerate(result.shape)]
        where[longest] = (where[longest] + shift) % result.shape[longest]
        spots.append(tuple(where))
    return result.at[spots[0]].set(smallest).at[spots[1]].set(high)


def levels(own_key, extent, cuts, smallest, high):
    loudness = 1.0
    for position, shards_of in cuts:
        steps = jax.random.uniform(jax.random.fold_in(jax.random.fold_in(own_key, 6), position), (shards_of,), jnp.float32, smallest / len(cuts), high / len(cuts))
        loudness = loudness * jnp.repeat(jnp.exp(steps), extent[position] // shards_of).reshape((-1,) + (1,) * (len(extent) - 1 - position))
    return loudness


def gaussian(own_key, dims, deviation, limit, pieces=(), kind=jnp.bfloat16):
    values = deviation * jax.random.normal(own_key, dims, jnp.float32)
    if pieces:
        values = values * levels(own_key, dims, pieces, -0.22, 0.18)
    return jnp.clip(values, -limit, limit).astype(kind)


def setup_inputs(seed: int = 0) -> dict:
    splits = jax.random.split(jax.random.key(seed), 14)
    map_thirteen = gaussian(splits[0], (IMGS, S16, S13, D), 1.0, 6.0, ((0, 4), (1, 16)))
    kv_cache = gaussian(splits[1], (IMGS, CACHE, 2, HEADS * HDIM), 1.0, 6.0, ((0, 4), (1, 16), (3, 4)))
    class_labels = touch_ends(jax.random.randint(splits[2], (IMGS,), 0, CLASSES), jax.random.fold_in(splits[2], 1), 0, CLASSES - 1).astype(jnp.int32)
    class_table = gaussian(splits[3], (CLASSES, 3, D), 1.0, 4.0, ((0, 4),))
    sampled_ids = touch_ends(jax.random.randint(splits[4], (IMGS, S13, S13), 0, VOCAB), jax.random.fold_in(splits[4], 1), 0, VOCAB - 1).astype(jnp.int32)
    codebook = gaussian(splits[5], (VOCAB, CDIM), 1.0, 6.0, (), jnp.float32)
    feature_sum = gaussian(splits[6], (IMGS, S16, S16 * CDIM), 1.0, 6.0, ((0, 4), (1, 16)), jnp.float32)
    embed_weight = gaussian(splits[7], (CDIM, D), CDIM ** -0.5, 1.0, (), jnp.float32)
    embed_bias = gaussian(splits[8], (D,), 0.5, 3.0, (), jnp.float32)
    position_table = gaussian(splits[9], (S16, S16, D), 0.5, 3.0, ((0, 16),))
    qkv_weight = gaussian(splits[10], (D, 3, HEADS * HDIM), D ** -0.5, 0.125, ((2, 4),))
    out_weight = gaussian(splits[11], (HEADS * HDIM, D), (HEADS * HDIM) ** -0.5, 0.1875, ((0, 4),))
    head_scale = jnp.clip(jnp.exp(math.log(40.0) - 2.9957323 * jax.random.uniform(splits[12], (HEADS,), jnp.float32) ** levels(splits[12], (HEADS,), ((0, 4),), -0.2, 0.2)), 2.0, 40.0)
    return {"map_thirteen": map_thirteen, "kv_cache": kv_cache, "class_labels": class_labels, "class_table": class_table, "sampled_ids": sampled_ids, "codebook": codebook, "feature_sum": feature_sum, "embed_weight": embed_weight, "embed_bias": embed_bias, "position_table": position_table, "qkv_weight": qkv_weight, "out_weight": out_weight, "head_scale": head_scale}


def upsample_table():
    source = (np.arange(S16) + 0.5) * S13 / S16 - 0.5
    source = np.maximum(source, 0.0)
    lower = np.floor(source).astype(np.int32)
    upper = np.minimum(lower + 1, S13 - 1)
    weight = source - lower
    interp = np.zeros((S16, S13))
    interp[np.arange(S16), lower] += 1.0 - weight
    interp[np.arange(S16), upper] += weight
    return interp

def normalize(vectors):
    return vectors * lax.rsqrt(lax.optimization_barrier(jnp.sum(vectors * vectors, axis=-1, keepdims=True)) + 1e-06)

def reference(map_thirteen, kv_cache, class_labels, class_table, sampled_ids, codebook, feature_sum, embed_weight, embed_bias, position_table, qkv_weight, out_weight, head_scale):
    width = HEADS * HDIM
    modulation = class_table[class_labels]
    interp = jnp.asarray(upsample_table(), jnp.float32)
    small_count = S16 * S13
    total_rows = small_count + S16 * S16
    query_ids = jnp.arange(total_rows, dtype=jnp.int32)
    key_ids = jnp.arange(CACHE + total_rows, dtype=jnp.int32)
    allowed = jnp.where(key_ids[None, :] < CACHE, key_ids[None, :] < COARSE, jnp.where(key_ids[None, :] < CACHE + small_count, (key_ids[None, :] - CACHE) // S13 < S13, query_ids[:, None] >= small_count))
    allowed = allowed.astype(jnp.float32)
    kept_rows = (jnp.arange(S16, dtype=jnp.int32) < S13)[:, None, None]

    def one_image(items):
        hidden, cached, modrows, indices, previous = items
        looked_up = codebook[indices]
        upsampled = jnp.einsum('ri,ijc->rjc', interp, looked_up, precision=lax.Precision.HIGHEST)
        upsampled = jnp.einsum('sj,rjc->rsc', interp, upsampled, precision=lax.Precision.HIGHEST)
        features = previous.reshape(S16, S16, CDIM) + upsampled
        embedded = jnp.dot(features.reshape(S16 * S16, CDIM), embed_weight, precision=lax.Precision.HIGHEST, preferred_element_type=jnp.float32)
        map_sixteen = (embedded + embed_bias + position_table.reshape(S16 * S16, D).astype(jnp.float32)).astype(jnp.bfloat16)
        inputs = jnp.concatenate([hidden.reshape(small_count, D), map_sixteen], axis=0).astype(jnp.float32)
        centred = inputs - lax.optimization_barrier(jnp.mean(inputs, axis=-1, keepdims=True))
        variance = lax.optimization_barrier(jnp.mean(centred * centred, axis=-1, keepdims=True))
        modf = modrows.astype(jnp.float32)
        modulated = (centred * lax.rsqrt(variance + 1e-06) * (1.0 + modf[1]) + modf[0]).astype(jnp.bfloat16)
        projected = jnp.dot(modulated, qkv_weight.reshape(D, 3 * width), preferred_element_type=jnp.float32)
        projected = projected.reshape(total_rows, 3, HEADS, HDIM)
        queries = (normalize(projected[:, 0]) * head_scale[None, :, None]).astype(jnp.bfloat16)
        keys = normalize(projected[:, 1]).astype(jnp.bfloat16)
        values = projected[:, 2].astype(jnp.bfloat16)
        cache_keys = normalize(cached[:, 0].astype(jnp.float32).reshape(CACHE, HEADS, HDIM)).astype(jnp.bfloat16)
        cache_values = cached[:, 1].reshape(CACHE, HEADS, HDIM)
        all_keys = jnp.concatenate([cache_keys, keys], axis=0)
        all_values = jnp.concatenate([cache_values, values], axis=0)
        scores = jnp.einsum('qhe,khe->hqk', queries.astype(jnp.float32), all_keys.astype(jnp.float32))
        weights = jnp.exp(scores) * allowed[None]
        denominator = lax.optimization_barrier(jnp.sum(weights, axis=-1))
        numerator = jnp.einsum('hqk,khe->qhe', weights.astype(jnp.bfloat16).astype(jnp.float32), all_values.astype(jnp.float32))
        attended = (numerator / denominator.T[:, :, None]).astype(jnp.bfloat16).reshape(total_rows, width)
        branch = jnp.dot(attended, out_weight, preferred_element_type=jnp.float32)
        gated = (modf[2] * branch).astype(jnp.bfloat16)
        branch_thirteen = gated[:small_count].reshape(S16, S13, D)
        branch_thirteen = jnp.where(kept_rows, branch_thirteen, jnp.zeros_like(branch_thirteen))
        branch_sixteen = gated[small_count:].reshape(S16, S16, D)
        return (branch_thirteen, branch_sixteen)
    branch_thirteen, branch_sixteen = lax.map(one_image, (map_thirteen, kv_cache, modulation, sampled_ids, feature_sum))
    return (branch_thirteen, branch_sixteen)
```

```python
import functools

import jax
import jax.numpy as jnp
from jax import lax
from jax.experimental import pallas as pl
from jax.experimental.pallas import tpu as pltpu
from jax.sharding import PartitionSpec as P

MESH = pl.DeviceIdType.MESH
S13 = 13
S16 = 16
D = 1920
W = 256
IMG = 8
HALF = 8
HEADSETS = 4
DPS = 4
TOK = 32
LARGE = IMG * S16
SMALL = IMG * S13
ROWS = 240
WIDE = 1024
SECOND = D - WIDE
F32 = jnp.float32
BF16 = jnp.bfloat16
VMEM_LIMIT = 58 * 1024 * 1024


def dot(a, b):
    return jnp.dot(a, b, preferred_element_type=F32)


def dot_nt(a, b):
    return lax.dot_general(a, b, (((1,), (1,)), ((), ())), preferred_element_type=F32)


def iota(shape, axis):
    return lax.broadcasted_iota(jnp.int32, shape, axis)


def flags(condition):
    return jnp.where(condition, 1.0, 0.0).astype(BF16)


def split(x):
    high = x.astype(BF16)
    return high, (x - high.astype(F32)).astype(BF16)


def layer_norm(x):
    centred = x - jnp.mean(x, axis=-1, keepdims=True)
    variance = jnp.mean(centred * centred, axis=-1, keepdims=True)
    return centred * lax.rsqrt(variance + 1e-06)


def remote(src, dst, send, recv, **device):
    return pltpu.make_async_remote_copy(
        src_ref=src, dst_ref=dst, send_sem=send, recv_sem=recv, device_id=device, device_id_type=MESH
    )


def kernel(
    labels, head_scale, ids, cache, feature_sum, bias, position,
    thirteen_hbm, table_hbm, codebook_hbm, embed_hbm, qkv_hbm, out_hbm,
    o13, o16,
    thirteen, table, codebook, embed, qkv, wout,
    cache_send, cache_recv, mod_a, mod_b, mod, feats, xhat, xmod,
    qkv_send, own_recv, other_recv, weights, vext, att_send, att_recv, att_all,
    local_sem,
    ma_s, ma_r, mb_s, mb_r, ca_s, ca_r, own_s, own_r, oth_s, oth_r, att_s, att_r,
    wz_s, wz_r, wy_s, wy_r, wx_s, wx_r, wc_s, wc_r,
):
    x = lax.axis_index("dp")
    seq = lax.axis_index("seq")
    h = lax.axis_index("head")
    zh, u = seq // HALF, seq % HALF
    y, core = u // 2, u % 2
    me = h * HALF + u

    def in_half(place):
        return zh * HALF + place

    def in_other(place):
        return (1 - zh) * HALF + place

    col0 = pl.multiple_of(u * W - (u // 7) * 128, 128)
    loads = [
        (table_hbm.at[:, :, pl.ds(col0, W)], table),
        (codebook_hbm, codebook),
        (embed_hbm, embed),
        (thirteen_hbm, thirteen),
        (out_hbm.at[:, pl.ds(0, WIDE)], wout.at[0, pl.ds(pl.multiple_of(h * W, W), W), :]),
        (out_hbm.at[:, pl.ds(SECOND, WIDE)], wout.at[1, pl.ds(pl.multiple_of(h * W, W), W), :]),
        (qkv_hbm, qkv),
    ]
    loads = [pltpu.make_async_copy(a, b, local_sem.at[i]) for i, (a, b) in enumerate(loads)]
    for load in loads:
        load.start()

    barrier = pltpu.get_barrier_semaphore()

    def greet_half(d, c):
        p = (me + d) % (HEADSETS * HALF)
        pl.semaphore_signal(
            barrier, inc=1, device_id={"seq": in_half(p % HALF), "head": p // HALF}, device_id_type=MESH
        )
        return c

    def greet_other(d, c):
        pl.semaphore_signal(
            barrier, inc=1, device_id={"seq": in_other((u + d) % HALF)}, device_id_type=MESH
        )
        return c

    def greet_dp(d, c):
        pl.semaphore_signal(barrier, inc=1, device_id={"dp": (x + d) % DPS}, device_id_type=MESH)
        return c

    lax.fori_loop(1, HEADSETS * HALF, greet_half, 0)
    lax.fori_loop(0, HALF, greet_other, 0)
    lax.fori_loop(1, DPS, greet_dp, 0)

    group = flags((iota((W, W), 0) >> 6) == (iota((W, W), 1) >> 6))

    def normalize(v):
        high, low = split(v * v)
        return v * lax.rsqrt(dot(high, group) + dot(low, group) + 1e-06)

    keys = cache[:, 0:16, :].reshape(IMG * 16, W).astype(F32)
    cache_send[:, 0:16, :] = normalize(keys).astype(BF16).reshape(IMG, 16, W)
    cache_send[:, 16:32, :] = cache[:, 16:32, :]

    loads[0].wait()
    owned = table.shape[1]
    rows8 = iota((IMG, owned), 0)
    wanted = jnp.zeros((IMG, owned), jnp.int32)
    for b in range(IMG):
        wanted = jnp.where(rows8 == b, labels[b] - h * owned, wanted)
    onehot = flags(wanted == iota((IMG, owned), 1))
    parts = [dot(onehot, table[t]) for t in range(3)] + [jnp.zeros((IMG, W), F32)]
    mod_a[h] = jnp.concatenate(parts, axis=0).astype(BF16)

    pl.semaphore_wait(barrier, HEADSETS * HALF - 1 + HALF + DPS - 1)

    def mod_a_copy(d):
        to = (h + d) % HEADSETS
        return remote(mod_a.at[h], mod_a.at[h], ma_s.at[to], ma_r.at[h], head=to)

    def mod_b_copy(d):
        to = (u + d) % HALF
        return remote(mod_b.at[u], mod_b.at[u], mb_s.at[to], mb_r.at[u], seq=in_half(to))

    def cache_copy(d):
        to = (seq + d) % 16
        return remote(cache_send.at[to % HALF], cache_recv.at[seq], ca_s.at[to], ca_r.at[seq], seq=to)

    def own_copy(d):
        to = (u + d) % HALF
        return remote(qkv_send.at[to], own_recv.at[u], own_s.at[to], own_r.at[u], seq=in_half(to))

    def other_copy(d):
        to = (u + d) % HALF
        return remote(
            qkv_send.at[to, pl.ds(TOK, 2 * TOK), :], other_recv.at[u], oth_s.at[to], oth_r.at[u],
            seq=in_other(to),
        )

    def att_copy(d):
        p = (me + d) % (HEADSETS * HALF)
        return remote(
            att_send.at[p % HALF], att_recv.at[h, u], att_s.at[p], att_r.at[me],
            seq=in_half(p % HALF), head=p // HALF,
        )

    def piece(part, start, count):
        return wout.at[core, pl.ds(pl.multiple_of(part * W + start, 16), count), :]

    def wz_copy(d):
        to = (h + d) % HEADSETS
        ref = piece(h, x * 64 + y * 16, 16)
        return remote(ref, ref, wz_s.at[to], wz_r.at[h], head=to)

    def wy_copy(i):
        to, part = (y + 1 + i // 3) % 4, (h + 1 + i % 3) % HEADSETS
        ref = piece(part, x * 64 + y * 16, 16)
        return remote(
            ref, ref, wy_s.at[to * 4 + part], wy_r.at[y * 4 + part], seq=in_half(to * 2 + core)
        )

    def wx_copy(i):
        to, part = (x + 1 + i // 3) % DPS, (h + 1 + i % 3) % HEADSETS
        ref = piece(part, x * 64, 64)
        return remote(ref, ref, wx_s.at[to * 4 + part], wx_r.at[x * 4 + part], dp=to)

    def wc_copy(i):
        part = (h + 1 + i) % HEADSETS
        ref = piece(part, 0, W)
        return remote(ref, ref, wc_s.at[part], wc_r.at[part], seq=in_half(u + 1 - 2 * core))

    def each(low, high, copy, action):
        def step(d, c):
            getattr(copy(d), action)()
            return c

        lax.fori_loop(low, high, step, 0)

    def arrived(low, high, ref_of, sem_of):
        def step(d, c):
            ref, sem = ref_of(d), sem_of(d)
            remote(ref, ref, ma_s.at[0], sem, head=(h + 1) % HEADSETS).wait_recv()
            return c

        lax.fori_loop(low, high, step, 0)

    each(1, HEADSETS, mod_a_copy, "start")
    loads[4].wait()
    loads[5].wait()
    each(1, HEADSETS, wz_copy, "start")
    each(1, 16, cache_copy, "start")
    cache_recv[seq] = cache_send[u]

    loads[1].wait()
    place = 26 * seq - 3 + 3 * ((16 - seq) // 16)
    lower = place // 32
    upper = lower + 1 - lower // (S13 - 1)
    weight = (place % 32).astype(F32) * (1.0 / 32.0)
    low_ids, high_ids = ids[lower], ids[upper]
    span = 512

    def look(c, total):
        start = pl.multiple_of(c * span, span)
        entry = iota((IMG, span), 1) + c * span
        hits = []
        for j in range(S13):
            hits.append(
                jnp.where(low_ids[:, j : j + 1] == entry, 1.0 - weight, 0.0)
                + jnp.where(high_ids[:, j : j + 1] == entry, weight, 0.0)
            )
        hits.append(jnp.zeros((IMG, span), F32))
        hits = jnp.concatenate(hits, axis=0).astype(BF16)
        high, low = split(codebook[:, pl.ds(start, span)])
        return total + dot_nt(hits, high) + dot_nt(hits, low)

    looked = lax.fori_loop(0, codebook.shape[1] // span, look, jnp.zeros((SMALL + IMG, 32), F32))
    for s in range(S16):
        at = max(26 * s - 3, 0)
        low = at // 32
        up = min(low + 1, S13 - 1)
        frac = (at % 32) / 32.0
        feats[s * IMG : (s + 1) * IMG, :] = (
            feature_sum[:, s * 32 : (s + 1) * 32]
            + looked[low * IMG : (low + 1) * IMG] * (1.0 - frac)
            + looked[up * IMG : (up + 1) * IMG] * frac
        )

    arrived(1, HEADSETS, lambda d: mod_a.at[(h + d) % HEADSETS], lambda d: ma_r.at[(h + d) % HEADSETS])
    total = mod_a[0].astype(F32)
    for part in range(1, HEADSETS):
        total = total + mod_a[part].astype(F32)
    mod_b[u] = total.astype(BF16)
    each(1, HALF, mod_b_copy, "start")

    loads[2].wait()
    feats_high, feats_low = split(feats[...])
    embed_high, embed_low = split(embed[...])
    xhat[0:LARGE, :] = dot(feats_high, embed_high) + dot(feats_high, embed_low) + dot(feats_low, embed_high)

    arrived(
        1, HEADSETS,
        lambda d: piece((h + d) % HEADSETS, x * 64 + y * 16, 16),
        lambda d: wz_r.at[(h + d) % HEADSETS],
    )
    each(0, 9, wy_copy, "start")

    for i in range(S16 // 2):
        table_rows = position[2 * i : 2 * i + 2, :].astype(F32)
        both = jnp.concatenate([jnp.broadcast_to(table_rows[k : k + 1], (IMG, D)) for k in range(2)], axis=0)
        rows = xhat[16 * i : 16 * i + 16, :] + bias[...] + both
        xhat[16 * i : 16 * i + 16, :] = layer_norm(rows.astype(BF16).astype(F32))
    loads[3].wait()
    for i in range(SMALL // 16):
        xhat[LARGE + 16 * i : LARGE + 16 * i + 16, :] = layer_norm(thirteen[16 * i : 16 * i + 16, :].astype(F32))
    xhat[LARGE + SMALL - 8 : LARGE + SMALL, :] = layer_norm(thirteen[SMALL - 8 : SMALL, :].astype(F32))
    xhat[LARGE + SMALL : ROWS, :] = jnp.zeros((ROWS - LARGE - SMALL, D), F32)

    arrived(1, HALF, lambda d: mod_b.at[(u + d) % HALF], lambda d: mb_r.at[(u + d) % HALF])
    for c in range(HALF):
        chunk = mod_b[c].astype(F32)
        if c == HALF - 1:
            chunk = chunk[:, 128:]
        width = chunk.shape[1]
        mod[0, :, c * W : c * W + width] = chunk[0:8]
        mod[1, :, c * W : c * W + width] = 1.0 + chunk[8:16]
        mod[2, :, c * W : c * W + width] = chunk[16:24]

    def modulate(i, carry):
        at = pl.multiple_of(i * 16, 16)
        rows = xhat[pl.ds(at, 16), :].reshape(2, IMG, D)
        rows = rows * mod[1][None] + mod[0][None]
        xmod[pl.ds(at, 16), :] = rows.reshape(16, D).astype(BF16)
        return carry

    lax.fori_loop(0, ROWS // 16, modulate, 0)

    loads[6].wait()
    r, c = iota((IMG * TOK, ROWS), 0), iota((IMG * TOK, ROWS), 1)
    token = r & (TOK - 1)
    to_image = flags((token < S13 + S16) & (c == token * IMG + (r >> 5)))
    lane_head = iota((1, W), 1) >> 6
    scales = jnp.zeros((1, W), F32)
    for k in range(4):
        scales = jnp.where(lane_head == k, head_scale[k], scales)
    for t in range(3):
        projected = dot(xmod[...], qkv[t])
        if t == 0:
            projected = normalize(projected) * scales
        elif t == 1:
            projected = normalize(projected)
        moved = dot(to_image, projected.astype(BF16)).astype(BF16)
        qkv_send[:, t * TOK : (t + 1) * TOK, :] = moved.reshape(IMG, TOK, W)
    each(0, HALF, other_copy, "start")
    each(1, HALF, own_copy, "start")
    own_recv[u] = qkv_send[u]

    def y_place(i):
        return (y + 1 + i // 3) % 4, (h + 1 + i % 3) % HEADSETS

    arrived(
        0, 9,
        lambda i: piece(y_place(i)[1], x * 64 + y_place(i)[0] * 16, 16),
        lambda i: wy_r.at[y_place(i)[0] * 4 + y_place(i)[1]],
    )
    each(0, 9, wx_copy, "start")

    arrived(1, 16, lambda d: cache_recv.at[(seq + d) % 16], lambda d: ca_r.at[(seq + d) % 16])
    arrived(1, HALF, lambda d: own_recv.at[(u + d) % HALF], lambda d: own_r.at[(u + d) % HALF])
    lanes = iota((W, W), 1) >> 6
    key = iota((W, W), 0)
    queries = own_recv[:, 0:TOK, :].reshape(W, W)
    masked = [jnp.where(lanes == k, queries, jnp.zeros_like(queries)) for k in range(4)]
    seen = jnp.where((iota((W, W), 0) & 31) >= S16, jnp.where((iota((W, W), 1) & 31) < S16, 0.0, 1.0), 1.0)

    def part(index, keys, values, valid, fine):
        for k in range(4):
            column = (index * 4 + k) * W
            scores = jnp.exp(dot_nt(masked[k], keys))
            if fine:
                scores = scores * seen
            weights[:, column : column + W] = scores.astype(BF16)
            use = valid & (lanes == k)
            vext[column : column + W, 0:W] = jnp.where(use, values, jnp.zeros_like(values))
            vext[column : column + W, W : 2 * W] = flags(use)

    def fine_valid(half):
        tok = key & 31
        return (tok < S16) | ((tok < S16 + S13) & (half * HALF + (key >> 5) < S13))

    part(
        0, cache_recv[:, 0:16, :].reshape(W, W), cache_recv[:, 16:32, :].reshape(W, W), key < W - 1, False
    )
    part(
        1, own_recv[:, TOK : 2 * TOK, :].reshape(W, W), own_recv[:, 2 * TOK : 3 * TOK, :].reshape(W, W),
        fine_valid(zh), True,
    )
    arrived(0, HALF, lambda d: other_recv.at[(u + d) % HALF], lambda d: oth_r.at[(u + d) % HALF])
    part(
        2, other_recv[:, 0:TOK, :].reshape(W, W), other_recv[:, TOK : 2 * TOK, :].reshape(W, W),
        fine_valid(1 - zh), True,
    )
    sums = dot(weights[...], vext[...])
    attended = (sums[:, 0:W] / sums[:, W : 2 * W]).astype(BF16)
    att_send[...] = attended.reshape(HALF, TOK, W)
    each(1, HEADSETS * HALF, att_copy, "start")
    att_recv[h, u] = att_send[u]

    def x_place(i):
        return (x + 1 + i // 3) % DPS, (h + 1 + i % 3) % HEADSETS

    arrived(
        0, 9,
        lambda i: piece(x_place(i)[1], x_place(i)[0] * 64, 64),
        lambda i: wx_r.at[x_place(i)[0] * 4 + x_place(i)[1]],
    )
    each(0, 3, wc_copy, "start")

    r, c = iota((ROWS, W), 0), iota((ROWS, W), 1)
    small = r - LARGE
    source = jnp.where(r < LARGE, (r >> 4) * TOK + (r & 15), (small & 7) * TOK + S16 + (small >> 3))
    to_row = flags(c == source)
    arrived(
        1, HEADSETS * HALF,
        lambda d: att_recv.at[((me + d) % (HEADSETS * HALF)) // HALF, (me + d) % HALF],
        lambda d: att_r.at[(me + d) % (HEADSETS * HALF)],
    )
    for k in range(HEADSETS):
        att_all[:, k * W : (k + 1) * W] = dot(to_row, att_recv[k].reshape(W, W)).astype(BF16)
    arrived(
        0, 3,
        lambda i: wout.at[1 - core, pl.ds(pl.multiple_of(((h + 1 + i) % HEADSETS) * W, W), W), :],
        lambda i: wc_r.at[(h + 1 + i) % HEADSETS],
    )
    kept = seq < S13
    for start in range(0, D, W):
        width = min(W, D - start)
        side = 0 if start < WIDE else 1
        first = start - side * SECOND
        branch = dot(att_all[...], wout[side, :, first : first + width])
        gate = mod[2, :, start : start + width]
        for b in range(IMG):
            o16[b, :, start : start + width] = (gate[b : b + 1] * branch[b * S16 : (b + 1) * S16]).astype(BF16)
        for j in range(S13):
            rows = gate * branch[LARGE + j * IMG : LARGE + (j + 1) * IMG]
            o13[j, :, start : start + width] = jnp.where(kept, rows, jnp.zeros_like(rows)).astype(BF16)

    each(1, HEADSETS, mod_a_copy, "wait_send")
    each(1, HALF, mod_b_copy, "wait_send")
    each(1, 16, cache_copy, "wait_send")
    each(1, HALF, own_copy, "wait_send")
    each(0, HALF, other_copy, "wait_send")
    each(1, HEADSETS * HALF, att_copy, "wait_send")
    each(1, HEADSETS, wz_copy, "wait_send")
    each(0, 9, wy_copy, "wait_send")
    each(0, 9, wx_copy, "wait_send")
    each(0, 3, wc_copy, "wait_send")


def body(
    map_thirteen, kv_cache, class_labels, class_table, sampled_ids, codebook, feature_sum,
    embed_weight, embed_bias, position_table, qkv_weight, out_weight, head_scale,
):
    owned = class_table.shape[0]
    vocabulary = codebook.shape[0]
    vmem = pl.BlockSpec(memory_space=pltpu.VMEM)
    smem = pl.BlockSpec(memory_space=pltpu.SMEM)
    anywhere = pl.BlockSpec(memory_space=pl.ANY)
    dma = pltpu.SemaphoreType.DMA
    o13, o16 = pl.pallas_call(
        kernel,
        out_shape=(
            jax.ShapeDtypeStruct((S13, IMG, D), BF16),
            jax.ShapeDtypeStruct((IMG, S16, D), BF16),
        ),
        in_specs=[smem, smem, vmem, vmem, vmem, vmem, vmem] + [anywhere] * 6,
        out_specs=(vmem, vmem),
        scratch_shapes=[
            pltpu.VMEM((SMALL, D), BF16),
            pltpu.VMEM((3, owned, W), BF16),
            pltpu.VMEM((32, vocabulary), F32),
            pltpu.VMEM((32, D), F32),
            pltpu.VMEM((3, D, W), BF16),
            pltpu.VMEM((2, HEADSETS * W, WIDE), BF16),
            pltpu.VMEM((IMG, 32, W), BF16),
            pltpu.VMEM((16, 32, W), BF16),
            pltpu.VMEM((HEADSETS, 32, W), BF16),
            pltpu.VMEM((HALF, 32, W), BF16),
            pltpu.VMEM((3, IMG, D), F32),
            pltpu.VMEM((LARGE, 32), F32),
            pltpu.VMEM((ROWS, D), F32),
            pltpu.VMEM((ROWS, D), BF16),
            pltpu.VMEM((IMG, 3 * TOK, W), BF16),
            pltpu.VMEM((HALF, 3 * TOK, W), BF16),
            pltpu.VMEM((HALF, 2 * TOK, W), BF16),
            pltpu.VMEM((W, 12 * W), BF16),
            pltpu.VMEM((12 * W, 2 * W), BF16),
            pltpu.VMEM((HALF, TOK, W), BF16),
            pltpu.VMEM((HEADSETS, HALF, TOK, W), BF16),
            pltpu.VMEM((ROWS, HEADSETS * W), BF16),
            dma((8,)),
        ]
        + [dma((n,)) for n in (4, 4, 8, 8, 16, 16, 8, 8, 8, 8, 32, 32, 4, 4, 16, 16, 16, 16, 4, 4)],
        compiler_params=pltpu.CompilerParams(
            collective_id=0, has_side_effects=True, vmem_limit_bytes=VMEM_LIMIT
        ),
        cost_estimate=pl.CostEstimate(flops=3_000_000_000, bytes_accessed=12_000_000, transcendentals=1_000_000),
    )(
        class_labels,
        head_scale,
        sampled_ids.transpose(1, 0, 2),
        kv_cache.transpose(0, 2, 1, 3).reshape(IMG, 32, W),
        feature_sum.reshape(IMG, S16 * 32),
        embed_bias.reshape(1, D),
        position_table.reshape(S16, D),
        map_thirteen.reshape(IMG, S13, D).transpose(1, 0, 2).reshape(SMALL, D),
        class_table.transpose(1, 0, 2),
        codebook.T,
        embed_weight,
        qkv_weight.transpose(1, 0, 2),
        out_weight,
    )
    return o13.transpose(1, 0, 2)[:, None], o16[:, None]


def solution(mesh):
    placed = (
        P("dp", "seq", None, None),
        P("dp", "seq", None, "head"),
        P("dp"),
        P("head", None, None),
        P("dp", None, None),
        P(),
        P("dp", "seq", None),
        P(),
        P(),
        P("seq", None, None),
        P(None, None, "head"),
        P("head", None),
        P("head"),
    )
    return jax.shard_map(
        body,
        mesh=mesh,
        in_specs=placed,
        out_specs=(P("dp", "seq", None, None), P("dp", "seq", None, None)),
        check_vma=False,
    )
```

```python
import functools

import jax
import jax.numpy as jnp
from jax import lax
from jax.experimental import pallas as pl
from jax.experimental.pallas import tpu as pltpu
from jax.sharding import PartitionSpec as P

MESH = pl.DeviceIdType.MESH
S13 = 13
S16 = 16
D = 1920
W = 256
IMG = 8
HALF = 8
HEADSETS = 4
DPS = 4
TOK = 16
LARGE = IMG * S16
SMALL = IMG * S13
PADDED = SMALL + IMG
ROWS = 2 * LARGE + PADDED
SPAN = 512
WIDE = 1024
SECOND = D - WIDE
F32 = jnp.float32
BF16 = jnp.bfloat16
VMEM_LIMIT = 58 * 1024 * 1024


def dot(a, b):
    return jnp.dot(a, b, preferred_element_type=F32)


def dot_nt(a, b):
    return lax.dot_general(a, b, (((1,), (1,)), ((), ())), preferred_element_type=F32)


def iota(shape, axis):
    return lax.broadcasted_iota(jnp.int32, shape, axis)


def flags(condition):
    return jnp.where(condition, 1.0, 0.0).astype(BF16)


def split(x):
    high = x.astype(BF16)
    return high, (x - high.astype(F32)).astype(BF16)


def layer_norm(x):
    centred = x - jnp.mean(x, axis=-1, keepdims=True)
    variance = jnp.mean(centred * centred, axis=-1, keepdims=True)
    return centred * lax.rsqrt(variance + 1e-06)


def remote(src, dst, send, recv, **device):
    return pltpu.make_async_remote_copy(
        src_ref=src, dst_ref=dst, send_sem=send, recv_sem=recv, device_id=device, device_id_type=MESH
    )


def kernel(
    labels, head_scale, ids, cache, feature_sum, bias, position,
    thirteen_hbm, table_hbm, codebook_hbm, embed_hbm, qkv_hbm, out_hbm,
    o13, o16,
    thirteen, table, codebook, embed, qkv, wout,
    cache_send, cache_recv, mod_a, mod_b, mod, far_position, far_features, id_lanes, xhat, xmod,
    small_send, small_near, small_far, large_send, large_near,
    weights, vext, att_small, att_large, small_recv, large_recv, small_all, large_all,
    local_sem,
    ma_s, ma_r, mb_s, mb_r, fp_s, fp_r, ca_s, ca_r, sn_s, sn_r, sf_s, sf_r, ln_s, ln_r,
    as_s, as_r, al_s, al_r, wz_s, wz_r, wy_s, wy_r, wx_s, wx_r, wc_s, wc_r,
):
    x = lax.axis_index("dp")
    seq = lax.axis_index("seq")
    h = lax.axis_index("head")
    zh, u = seq // HALF, seq % HALF
    y, core = u // 2, u % 2
    me = h * HALF + u

    def in_half(place):
        return zh * HALF + place

    def in_other(place):
        return (1 - zh) * HALF + place

    col0 = pl.multiple_of(u * W - (u // 7) * 128, 128)
    loads = [
        (table_hbm.at[:, :, pl.ds(col0, W)], table),
        (codebook_hbm, codebook),
        (embed_hbm, embed),
        (thirteen_hbm, thirteen),
        (out_hbm.at[:, pl.ds(0, WIDE)], wout.at[0, pl.ds(pl.multiple_of(h * W, W), W), :]),
        (out_hbm.at[:, pl.ds(SECOND, WIDE)], wout.at[1, pl.ds(pl.multiple_of(h * W, W), W), :]),
        (qkv_hbm, qkv),
    ]
    loads = [pltpu.make_async_copy(a, b, local_sem.at[i]) for i, (a, b) in enumerate(loads)]
    for load in loads:
        load.start()

    barrier = pltpu.get_barrier_semaphore()

    def greet_half(d, c):
        p = (me + d) % (HEADSETS * HALF)
        pl.semaphore_signal(
            barrier, inc=1, device_id={"seq": in_half(p % HALF), "head": p // HALF}, device_id_type=MESH
        )
        return c

    def greet_other(d, c):
        pl.semaphore_signal(
            barrier, inc=1, device_id={"seq": in_other((u + d) % HALF)}, device_id_type=MESH
        )
        return c

    def greet_dp(d, c):
        pl.semaphore_signal(barrier, inc=1, device_id={"dp": (x + d) % DPS}, device_id_type=MESH)
        return c

    lax.fori_loop(1, HEADSETS * HALF, greet_half, 0)
    lax.fori_loop(0, HALF, greet_other, 0)
    lax.fori_loop(1, DPS, greet_dp, 0)

    def mod_a_copy(d):
        to = (h + d) % HEADSETS
        return remote(mod_a.at[h], mod_a.at[h], ma_s.at[to], ma_r.at[h], head=to)

    def mod_b_copy(d):
        to = (u + d) % HALF
        return remote(mod_b.at[u], mod_b.at[u], mb_s.at[to], mb_r.at[u], seq=in_half(to))

    def cache_copy(d):
        to = (seq + d) % 16
        return remote(cache_send.at[to % HALF], cache_recv.at[seq], ca_s.at[to], ca_r.at[seq], seq=to)

    def small_near_copy(d):
        to = (u + d) % HALF
        return remote(small_send.at[to], small_near.at[u], sn_s.at[to], sn_r.at[u], seq=in_half(to))

    def small_far_copy(d):
        to = (u + d) % HALF
        return remote(
            small_send.at[to, pl.ds(TOK, 2 * TOK), :], small_far.at[u], sf_s.at[to], sf_r.at[u],
            seq=in_other(to),
        )

    def large_near_copy(d):
        to = (u + d) % HALF
        return remote(large_send.at[to], large_near.at[u], ln_s.at[to], ln_r.at[u], seq=in_half(to))

    def peer(d):
        return (me + d) % (HEADSETS * HALF)

    def att_copy(source, target, send, recv):
        def copy(d):
            p = peer(d)
            return remote(
                source.at[p % HALF], target.at[h, u], send.at[p], recv.at[me],
                seq=in_half(p % HALF), head=p // HALF,
            )

        return copy

    def piece(side, part, start, count):
        return wout.at[side, pl.ds(pl.multiple_of(part * W + start, 16), count), :]

    def wz_copy(d):
        to = (h + d) % HEADSETS
        ref = piece(core, h, x * 64 + y * 16, 16)
        return remote(ref, ref, wz_s.at[to], wz_r.at[h], head=to)

    def y_place(i):
        return (y + 1 + i // 3) % 4, (h + 1 + i % 3) % HEADSETS

    def wy_copy(i):
        to, part = y_place(i)
        ref = piece(core, part, x * 64 + y * 16, 16)
        return remote(
            ref, ref, wy_s.at[to * 4 + part], wy_r.at[y * 4 + part], seq=in_half(to * 2 + core)
        )

    def x_place(i):
        return (x + i // 3) % DPS, (h + 1 + i % 3) % HEADSETS

    def wx_copy(i):
        to, part = x_place(i)
        ref = piece(core, part, x * 64, 64)
        return remote(ref, ref, wx_s.at[to * 4 + part], wx_r.at[x * 4 + part], dp=to)

    def wc_copy(i):
        at, part = x_place(i)
        ref = piece(core, part, at * 64, 64)
        return remote(
            ref, ref, wc_s.at[at * 4 + part], wc_r.at[at * 4 + part], seq=in_half(u + 1 - 2 * core)
        )

    def x_arrival(i):
        return piece(core, x_place(i)[1], x_place(i)[0] * 64, 64), wx_r.at[x_place(i)[0] * 4 + x_place(i)[1]]

    def c_arrival(i):
        return (
            piece(1 - core, x_place(i)[1], x_place(i)[0] * 64, 64),
            wc_r.at[x_place(i)[0] * 4 + x_place(i)[1]],
        )

    groups = {
        "mod_a": (1, HEADSETS, mod_a_copy, lambda d: (mod_a.at[(h + d) % HEADSETS], ma_r.at[(h + d) % HEADSETS])),
        "mod_b": (1, HALF, mod_b_copy, lambda d: (mod_b.at[(u + d) % HALF], mb_r.at[(u + d) % HALF])),
        "cache": (1, 16, cache_copy, lambda d: (cache_recv.at[(seq + d) % 16], ca_r.at[(seq + d) % 16])),
        "small_near": (
            1, HALF, small_near_copy, lambda d: (small_near.at[(u + d) % HALF], sn_r.at[(u + d) % HALF]),
        ),
        "small_far": (
            0, HALF, small_far_copy, lambda d: (small_far.at[(u + d) % HALF], sf_r.at[(u + d) % HALF]),
        ),
        "large_near": (
            1, HALF, large_near_copy, lambda d: (large_near.at[(u + d) % HALF], ln_r.at[(u + d) % HALF]),
        ),
        "att_small": (
            1, HEADSETS * HALF, att_copy(att_small, small_recv, as_s, as_r),
            lambda d: (small_recv.at[peer(d) // HALF, peer(d) % HALF], as_r.at[peer(d)]),
        ),
        "att_large": (
            1, HEADSETS * HALF, att_copy(att_large, large_recv, al_s, al_r),
            lambda d: (large_recv.at[peer(d) // HALF, peer(d) % HALF], al_r.at[peer(d)]),
        ),
        "wz": (
            1, HEADSETS, wz_copy,
            lambda d: (piece(core, (h + d) % HEADSETS, x * 64 + y * 16, 16), wz_r.at[(h + d) % HEADSETS]),
        ),
        "wy": (
            0, 9, wy_copy,
            lambda i: (
                piece(core, y_place(i)[1], x * 64 + y_place(i)[0] * 16, 16),
                wy_r.at[y_place(i)[0] * 4 + y_place(i)[1]],
            ),
        ),
        "wx": (3, 12, wx_copy, x_arrival),
        "wc": (0, 12, wc_copy, c_arrival),
    }

    def over(low, high, action):
        def step(d, c):
            action(d)
            return c

        lax.fori_loop(low, high, step, 0)

    def landed(place):
        slot, sem = place
        remote(slot, slot, ma_s.at[0], sem, head=(h + 1) % HEADSETS).wait_recv()

    def start(name):
        low, high, copy, _ = groups[name]
        over(low, high, lambda d: copy(d).start())

    def arrive(name):
        low, high, _, arrival = groups[name]
        over(low, high, lambda d: landed(arrival(d)))

    def sent(name):
        low, high, copy, _ = groups[name]
        over(low, high, lambda d: copy(d).wait_send())

    partner = [
        remote(position.at[0], far_position, fp_s.at[0], fp_r.at[0], seq=in_other(u)),
        remote(feature_sum, far_features, fp_s.at[1], fp_r.at[1], seq=in_other(u)),
    ]

    loads[0].wait()
    owned = table.shape[1]
    rows8 = iota((IMG, owned), 0)
    wanted = jnp.zeros((IMG, owned), jnp.int32)
    for b in range(IMG):
        wanted = jnp.where(rows8 == b, labels[b] - h * owned, wanted)
    onehot = flags(wanted == iota((IMG, owned), 1))
    parts = [dot(onehot, table[t]) for t in range(3)] + [jnp.zeros((IMG, W), F32)]
    mod_a[h] = jnp.concatenate(parts, axis=0).astype(BF16)

    pl.semaphore_wait(barrier, HEADSETS * HALF - 1 + HALF + DPS - 1)
    start("mod_a")
    for copy in partner:
        copy.start()

    group = flags((iota((W, W), 0) >> 6) == (iota((W, W), 1) >> 6))

    def normalize(v):
        high, low = split(v * v)
        return v * lax.rsqrt(dot(high, group) + dot(low, group) + 1e-06)

    r, c = iota((W, W), 0), iota((W, W), 1)
    to_kind = flags(c == ((r >> 5) * 32 + (r & 15) * 2 + ((r >> 4) & 1)))
    moved = dot(to_kind, cache[...].reshape(W, W))
    moved = jnp.where(((r >> 4) & 1) == 0, normalize(moved), moved)
    cache_send[...] = moved.astype(BF16).reshape(IMG, 32, W)
    cache_recv[seq] = cache_send[u]

    loads[4].wait()
    loads[5].wait()
    start("wz")

    taps = []
    for n, row in enumerate((seq, (seq + HALF) % 16)):
        place = 26 * row - 3 + 3 * ((16 - row) // 16)
        lower = place // 32
        upper = lower + 1 - lower // (S13 - 1)
        taps.append((place % 32).astype(F32) * (1.0 / 32.0))
        for t, source in enumerate((ids[lower], ids[upper])):
            for j in range(S13):
                id_lanes[2 * n + t, j] = jnp.broadcast_to(source[:, j : j + 1], (IMG, 128))
    loads[1].wait()

    def look(c, total):
        start_at = pl.multiple_of(c * SPAN, SPAN)
        columns = []
        for q in range(SPAN // 128):
            entry = iota((IMG, 128), 1) + (c * SPAN + q * 128)
            hits = []
            for n in range(2):
                for j in range(S13):
                    hits.append(
                        jnp.where(id_lanes[2 * n, j] == entry, 1.0 - taps[n], 0.0)
                        + jnp.where(id_lanes[2 * n + 1, j] == entry, taps[n], 0.0)
                    )
            columns.append(jnp.concatenate(hits, axis=0).astype(BF16))
        both = jnp.concatenate(split(codebook[:, pl.ds(start_at, SPAN)]), axis=0)
        return total + dot_nt(jnp.concatenate(columns, axis=1), both)

    looked = lax.fori_loop(0, codebook.shape[1] // SPAN, look, jnp.zeros((2 * SMALL, 64), F32))
    looked = looked[:, 0:32] + looked[:, 32:64]

    arrive("mod_a")
    total = mod_a[0].astype(F32)
    for part in range(1, HEADSETS):
        total = total + mod_a[part].astype(F32)
    mod_b[u] = total.astype(BF16)
    start("mod_b")
    start("cache")

    loads[3].wait()
    first = 2 * LARGE
    for i in range(SMALL // 16):
        xhat[first + 16 * i : first + 16 * i + 16, :] = layer_norm(thirteen[16 * i : 16 * i + 16, :].astype(F32))
    xhat[ROWS - 16 : ROWS - 8, :] = layer_norm(thirteen[SMALL - 8 : SMALL, :].astype(F32))
    xhat[ROWS - 8 : ROWS, :] = jnp.zeros((8, D), F32)
    arrive("wz")
    start("wy")
    loads[2].wait()
    embed_high, embed_low = split(embed[...])
    embed_parts = jnp.concatenate([embed_high, embed_low, embed_high], axis=0)
    bias_row = bias[...].reshape(1, D)

    def embedded(first, source, rows, table_rows):
        features = []
        for s in range(S16):
            at = max(26 * s - 3, 0)
            low = at // 32
            up = min(low + 1, S13 - 1)
            frac = (at % 32) / 32.0
            features.append(
                source[:, s * 32 : (s + 1) * 32]
                + rows[low * IMG : (low + 1) * IMG] * (1.0 - frac)
                + rows[up * IMG : (up + 1) * IMG] * frac
            )
        high, low = split(jnp.concatenate(features, axis=0))
        xhat[first : first + LARGE, :] = dot(jnp.concatenate([high, high, low], axis=1), embed_parts)
        for i in range(S16 // 2):
            pair = table_rows[2 * i : 2 * i + 2, :].astype(F32)
            pair = jnp.concatenate([jnp.broadcast_to(pair[k : k + 1], (IMG, D)) for k in range(2)], axis=0)
            at = first + 16 * i
            row = xhat[at : at + 16, :] + bias_row + pair
            xhat[at : at + 16, :] = layer_norm(row.astype(BF16).astype(F32))

    embedded(0, feature_sum[:, 0, :], looked[0:SMALL], position[0])
    for copy in partner:
        copy.wait_recv()
    embedded(LARGE, far_features[:, 0, :], looked[SMALL : 2 * SMALL], far_position[...])

    arrive("mod_b")
    for c in range(HALF):
        chunk = mod_b[c].astype(F32)
        if c == HALF - 1:
            chunk = chunk[:, 128:]
        width = chunk.shape[1]
        mod[0, :, c * W : c * W + width] = chunk[0:8]
        mod[1, :, c * W : c * W + width] = 1.0 + chunk[8:16]
        mod[2, :, c * W : c * W + width] = chunk[16:24]

    def modulate(i):
        at = pl.multiple_of(i * 16, 16)
        rows = xhat[pl.ds(at, 16), :].reshape(2, IMG, D)
        rows = rows * mod[1][None] + mod[0][None]
        xmod[pl.ds(at, 16), :] = rows.reshape(16, D).astype(BF16)

    lane_head = iota((1, W), 1) >> 6
    scales = jnp.zeros((1, W), F32)
    for k in range(4):
        scales = jnp.where(lane_head == k, head_scale[k], scales)

    def project(first, count, t):
        out = dot(xmod[first : first + count, :], qkv[t])
        if t == 0:
            out = normalize(out) * scales
        elif t == 1:
            out = normalize(out)
        return out.astype(BF16)

    over(2 * LARGE // 16, ROWS // 16, modulate)
    loads[6].wait()
    r, c = iota((LARGE, PADDED), 0), iota((LARGE, PADDED), 1)
    to_image = flags(((r & 15) < S13) & (c == (r & 15) * IMG + (r >> 4)))
    for t in (1, 2, 0):
        moved = dot(to_image, project(2 * LARGE, PADDED, t)).astype(BF16)
        small_send[:, t * TOK : (t + 1) * TOK, :] = moved.reshape(IMG, TOK, W)
        if t == 2:
            start("small_far")
    start("small_near")
    small_near[u] = small_send[u]

    over(0, 2 * LARGE // 16, modulate)
    r, c = iota((LARGE, LARGE), 0), iota((LARGE, LARGE), 1)
    to_image = flags(c == (r & 15) * IMG + (r >> 4))
    slot = 0
    for t, first in ((0, 0), (1, 0), (2, 0), (1, LARGE), (2, LARGE)):
        moved = dot(to_image, project(first, LARGE, t)).astype(BF16)
        large_send[:, slot * TOK : (slot + 1) * TOK, :] = moved.reshape(IMG, TOK, W)
        slot += 1
    start("large_near")
    large_near[u] = large_send[u]

    arrive("wy")
    start("wx")
    over(0, 3, lambda i: wc_copy(i).start())

    lanes = iota((W, W), 1) >> 6
    key = iota((W, W), 0)

    def by_head(rows):
        return [
            jnp.where(lanes[0:LARGE] == k, rows, jnp.zeros_like(rows)) for k in range(4)
        ]

    def offer(index, values, valid):
        for k in range(4):
            row = (index * 4 + k) * W
            use = lanes == k
            if valid is not None:
                use = use & valid
            vext[row : row + W, 0:W] = jnp.where(use, values, jnp.zeros_like(values))
            vext[row : row + W, W : 2 * W] = flags(use)

    def weigh(index, queries, keys):
        for k in range(4):
            column = (index * 4 + k) * W
            weights[:, column : column + W] = jnp.exp(dot_nt(queries[k], keys)).astype(BF16)

    def attend(queries, keys, out):
        for index, block in enumerate(keys):
            weigh(index, queries, block)
        used = len(keys) * 4 * W
        sums = dot(weights[:, 0:used], vext[0:used, :])
        out[...] = (sums[:, 0:W] / sums[:, W : 2 * W]).astype(BF16).reshape(HALF, TOK, W)

    arrive("cache")
    cache_keys = cache_recv[:, 0:16, :].reshape(W, W)
    offer(0, cache_recv[:, 16:32, :].reshape(W, W), key < W - 1)
    arrive("small_near")
    arrive("small_far")
    small_keys = jnp.concatenate(
        [small_near[:, TOK : 2 * TOK, :].reshape(LARGE, W), small_far[:, 0:TOK, :].reshape(LARGE, W)], axis=0
    )
    small_values = jnp.concatenate(
        [small_near[:, 2 * TOK : 3 * TOK, :].reshape(LARGE, W), small_far[:, TOK : 2 * TOK, :].reshape(LARGE, W)],
        axis=0,
    )
    map_row = (key >> 4) + HALF * zh * jnp.where(key < LARGE, 1, -1)
    offer(1, small_values, ((key & 15) < S13) & (map_row < S13))
    attend(by_head(small_near[:, 0:TOK, :].reshape(LARGE, W)), [cache_keys, small_keys], att_small)
    start("att_small")
    small_recv[h, u] = att_small[u]

    arrive("large_near")
    large_keys = jnp.concatenate(
        [large_near[:, k * TOK : (k + 1) * TOK, :].reshape(LARGE, W) for k in (1, 3)], axis=0
    )
    large_values = jnp.concatenate(
        [large_near[:, k * TOK : (k + 1) * TOK, :].reshape(LARGE, W) for k in (2, 4)], axis=0
    )
    offer(2, large_values, None)
    attend(
        by_head(large_near[:, 0:TOK, :].reshape(LARGE, W)), [cache_keys, small_keys, large_keys], att_large
    )
    start("att_large")
    large_recv[h, u] = att_large[u]

    def pass_on(i):
        landed(x_arrival(i))
        wc_copy(i).start()

    over(3, 12, pass_on)

    def columns():
        for first in range(0, D, W):
            width = min(W, D - first)
            side = 0 if first < WIDE else 1
            inner = first - side * SECOND
            yield first, first + width, wout.at[side, :, inner : inner + width]

    r, c = iota((PADDED, LARGE), 0), iota((PADDED, LARGE), 1)
    to_row = flags(c == (r & 7) * TOK + (r >> 3))
    arrive("att_small")
    for k in range(HEADSETS):
        small_all[:, k * W : (k + 1) * W] = dot(to_row, small_recv[k].reshape(LARGE, W)).astype(BF16)
    arrive("wc")
    kept = seq < S13
    for low, high, block in columns():
        branch = dot(small_all[...], block[...])
        gate = mod[2, :, low:high]
        for j in range(S13):
            rows = gate * branch[j * IMG : (j + 1) * IMG]
            o13[j, :, low:high] = jnp.where(kept, rows, jnp.zeros_like(rows)).astype(BF16)
    arrive("att_large")
    for k in range(HEADSETS):
        large_all[:, k * W : (k + 1) * W] = large_recv[k].reshape(LARGE, W)
    for low, high, block in columns():
        branch = dot(large_all[...], block[...])
        gate = mod[2, :, low:high]
        for b in range(IMG):
            o16[b, :, low:high] = (gate[b : b + 1] * branch[b * S16 : (b + 1) * S16]).astype(BF16)

    for copy in partner:
        copy.wait_send()
    for name in groups:
        sent(name)


def body(
    map_thirteen, kv_cache, class_labels, class_table, sampled_ids, codebook, feature_sum,
    embed_weight, embed_bias, position_table, qkv_weight, out_weight, head_scale,
):
    owned = class_table.shape[0]
    vocabulary = codebook.shape[0]
    vmem = pl.BlockSpec(memory_space=pltpu.VMEM)
    smem = pl.BlockSpec(memory_space=pltpu.SMEM)
    anywhere = pl.BlockSpec(memory_space=pl.ANY)
    dma = pltpu.SemaphoreType.DMA
    o13, o16 = pl.pallas_call(
        kernel,
        out_shape=(
            jax.ShapeDtypeStruct((S13, IMG, D), BF16),
            jax.ShapeDtypeStruct((IMG, S16, D), BF16),
        ),
        in_specs=[smem, smem, vmem, vmem, vmem, vmem, vmem] + [anywhere] * 6,
        out_specs=(vmem, vmem),
        scratch_shapes=[
            pltpu.VMEM((SMALL, D), BF16),
            pltpu.VMEM((3, owned, W), BF16),
            pltpu.VMEM((32, vocabulary), F32),
            pltpu.VMEM((32, D), F32),
            pltpu.VMEM((3, D, W), BF16),
            pltpu.VMEM((2, HEADSETS * W, WIDE), BF16),
            pltpu.VMEM((IMG, 32, W), BF16),
            pltpu.VMEM((16, 32, W), BF16),
            pltpu.VMEM((HEADSETS, 32, W), BF16),
            pltpu.VMEM((HALF, 32, W), BF16),
            pltpu.VMEM((3, IMG, D), F32),
            pltpu.VMEM((S16, D), BF16),
            pltpu.VMEM((IMG, 1, S16 * 32), F32),
            pltpu.VMEM((4, S13, IMG, 128), jnp.int32),
            pltpu.VMEM((ROWS, D), F32),
            pltpu.VMEM((ROWS, D), BF16),
            pltpu.VMEM((IMG, 3 * TOK, W), BF16),
            pltpu.VMEM((HALF, 3 * TOK, W), BF16),
            pltpu.VMEM((HALF, 2 * TOK, W), BF16),
            pltpu.VMEM((IMG, 5 * TOK, W), BF16),
            pltpu.VMEM((HALF, 5 * TOK, W), BF16),
            pltpu.VMEM((LARGE, 12 * W), BF16),
            pltpu.VMEM((12 * W, 2 * W), BF16),
            pltpu.VMEM((HALF, TOK, W), BF16),
            pltpu.VMEM((HALF, TOK, W), BF16),
            pltpu.VMEM((HEADSETS, HALF, TOK, W), BF16),
            pltpu.VMEM((HEADSETS, HALF, TOK, W), BF16),
            pltpu.VMEM((PADDED, HEADSETS * W), BF16),
            pltpu.VMEM((LARGE, HEADSETS * W), BF16),
            dma((8,)),
        ]
        + [dma((n,)) for n in (4, 4, 8, 8, 2, 2, 16, 16, 8, 8, 8, 8, 8, 8, 32, 32, 32, 32, 4, 4, 16, 16, 16, 16, 16, 16)],
        compiler_params=pltpu.CompilerParams(
            collective_id=0, has_side_effects=True, vmem_limit_bytes=VMEM_LIMIT
        ),
        cost_estimate=pl.CostEstimate(flops=3_000_000_000, bytes_accessed=12_000_000, transcendentals=1_000_000),
    )(
        class_labels,
        head_scale,
        sampled_ids.transpose(1, 0, 2),
        kv_cache,
        feature_sum,
        embed_bias,
        position_table,
        map_thirteen.reshape(IMG, S13, D).transpose(1, 0, 2).reshape(SMALL, D),
        class_table.transpose(1, 0, 2),
        codebook.T,
        embed_weight,
        qkv_weight.transpose(1, 0, 2),
        out_weight,
    )
    return o13.transpose(1, 0, 2)[:, None], o16[:, None]


def solution(mesh):
    placed = (
        P("dp", "seq", None, None),
        P("dp", "seq", None, "head"),
        P("dp"),
        P("head", None, None),
        P("dp", None, None),
        P(),
        P("dp", "seq", None),
        P(),
        P(),
        P("seq", None, None),
        P(None, None, "head"),
        P("head", None),
        P("head"),
    )
    return jax.shard_map(
        body,
        mesh=mesh,
        in_specs=placed,
        out_specs=(P("dp", "seq", None, None), P("dp", "seq", None, None)),
        check_vma=False,
    )
```

```python
import functools

import jax
import jax.numpy as jnp
from jax import lax
from jax.experimental import pallas as pl
from jax.experimental.pallas import tpu as pltpu
from jax.sharding import PartitionSpec as P

MESH = pl.DeviceIdType.MESH
S13 = 13
S16 = 16
D = 1920
W = 256
IMG = 8
HALF = 8
HEADSETS = 4
DPS = 4
TOK = 16
LARGE = IMG * S16
SMALL = IMG * S13
PADDED = SMALL + IMG
ROWS = 2 * LARGE + PADDED
SPAN = 512
VIA_X = 768
WIDE = 1024
SECOND = D - WIDE
F32 = jnp.float32
BF16 = jnp.bfloat16
VMEM_LIMIT = 58 * 1024 * 1024


def dot(a, b):
    return jnp.dot(a, b, preferred_element_type=F32)


def dot_nt(a, b):
    return lax.dot_general(a, b, (((1,), (1,)), ((), ())), preferred_element_type=F32)


def iota(shape, axis):
    return lax.broadcasted_iota(jnp.int32, shape, axis)


def flags(condition):
    return jnp.where(condition, 1.0, 0.0).astype(BF16)


def split(x):
    high = x.astype(BF16)
    return high, (x - high.astype(F32)).astype(BF16)


def layer_norm(x):
    centred = x - jnp.mean(x, axis=-1, keepdims=True)
    variance = jnp.mean(centred * centred, axis=-1, keepdims=True)
    return centred * lax.rsqrt(variance + 1e-06)


def remote(src, dst, send, recv, **device):
    return pltpu.make_async_remote_copy(
        src_ref=src, dst_ref=dst, send_sem=send, recv_sem=recv, device_id=device, device_id_type=MESH
    )


def kernel(
    labels_hbm, scale_hbm, ids_hbm, cache_hbm, features_hbm, bias_hbm, position_hbm,
    thirteen_hbm, table_hbm, codebook_hbm, embed_hbm, qkv_hbm, out_hbm,
    o13, o16,
    labels, head_scale, ids, cache, feature_sum, bias, position,
    thirteen, table, codebook, embed, qkv, wout,
    cache_send, cache_recv, mod_a, mod_b, mod, far_position, far_features, id_lanes, xhat, xmod,
    small_send, small_near, small_far, large_send, large_near,
    weights, vext, att_small, att_large, small_recv, large_recv, small_all, large_all,
    local_sem,
    ma_s, ma_r, mb_s, mb_r, fp_s, fp_r, ca_s, ca_r, sn_s, sn_r, sf_s, sf_r, ln_s, ln_r,
    as_s, as_r, al_s, al_r, fs_s, fl_s,
    wz_s, wz_r, ay_s, ay_r, bx_s, bx_r, ax_s, ax_r, by_s, by_r, wc_s, wc_r,
):
    x = lax.axis_index("dp")
    seq = lax.axis_index("seq")
    h = lax.axis_index("head")
    zh, u = seq // HALF, seq % HALF
    y, core = u // 2, u % 2
    me = h * HALF + u

    def in_half(place):
        return zh * HALF + place

    def in_other(place):
        return (1 - zh) * HALF + place

    barrier = pltpu.get_barrier_semaphore()

    def greet_half(d, c):
        p = (me + d) % (HEADSETS * HALF)
        pl.semaphore_signal(
            barrier, inc=1, device_id={"seq": in_half(p % HALF), "head": p // HALF}, device_id_type=MESH
        )
        return c

    def greet_other(d, c):
        pl.semaphore_signal(
            barrier, inc=1, device_id={"seq": in_other((u + d) % HALF)}, device_id_type=MESH
        )
        return c

    def greet_dp(d, c):
        pl.semaphore_signal(barrier, inc=1, device_id={"dp": (x + d) % DPS}, device_id_type=MESH)
        return c

    lax.fori_loop(0, HALF, greet_other, 0)
    lax.fori_loop(1, HEADSETS * HALF, greet_half, 0)
    lax.fori_loop(1, DPS, greet_dp, 0)

    col0 = pl.multiple_of(u * W - (u // 7) * 128, 128)
    loads = [
        (labels_hbm, labels),
        (table_hbm.at[:, :, pl.ds(col0, W)], table),
        (cache_hbm, cache),
        (position_hbm, position),
        (features_hbm, feature_sum),
        (ids_hbm, ids),
        (codebook_hbm, codebook),
        (out_hbm.at[:, pl.ds(0, WIDE)], wout.at[0, pl.ds(pl.multiple_of(h * W, W), W), :]),
        (out_hbm.at[:, pl.ds(SECOND, WIDE)], wout.at[1, pl.ds(pl.multiple_of(h * W, W), W), :]),
        (thirteen_hbm, thirteen),
        (embed_hbm, embed),
        (bias_hbm, bias),
        (scale_hbm, head_scale),
        (qkv_hbm, qkv),
    ]
    names = (
        "labels", "table", "cache", "position", "features", "ids", "codebook", "out0", "out1", "thirteen",
        "embed", "bias", "scale", "qkv",
    )
    loads = {
        name: pltpu.make_async_copy(a, b, local_sem.at[i]) for i, (name, (a, b)) in enumerate(zip(names, loads))
    }
    for load in loads.values():
        load.start()

    def mod_a_copy(d):
        to = (h + d) % HEADSETS
        return remote(mod_a.at[h], mod_a.at[h], ma_s.at[to], ma_r.at[h], head=to)

    def mod_b_copy(d):
        to = (u + d) % HALF
        return remote(mod_b.at[u], mod_b.at[u], mb_s.at[to], mb_r.at[u], seq=in_half(to))

    def cache_copy(d):
        to = (seq + d) % 16
        return remote(cache_send.at[to % HALF], cache_recv.at[seq], ca_s.at[to], ca_r.at[seq], seq=to)

    def small_near_copy(d):
        to = (u + d) % HALF
        return remote(small_send.at[to], small_near.at[u], sn_s.at[to], sn_r.at[u], seq=in_half(to))

    def small_far_copy(d):
        to = (u + d) % HALF
        return remote(
            small_send.at[to, pl.ds(TOK, 2 * TOK), :], small_far.at[u], sf_s.at[to], sf_r.at[u],
            seq=in_other(to),
        )

    def large_near_copy(d):
        to = (u + d) % HALF
        return remote(large_send.at[to], large_near.at[u], ln_s.at[to], ln_r.at[u], seq=in_half(to))

    def peer(d):
        return (me + d) % (HEADSETS * HALF)

    relay = (h % 3) > 0
    relayed, beyond = 3 * (2 - h), 3 * (h - 1)

    class Gather:
        def __init__(self, source, target, send, recv, forward):
            self.source, self.target, self.send, self.recv, self.forward = source, target, send, recv, forward

        def copy(self, p):
            return remote(
                self.source.at[p % HALF], self.target.at[h, u], self.send.at[p], self.recv.at[me],
                seq=in_half(p % HALF), head=p // HALF,
            )

        def direct(self, action):
            def step(d):
                p = peer(d)

                getattr(self.copy(p), action)()

            over(1, HEADSETS * HALF, step)

        def start(self):
            self.direct("start")
            self.target[h, u] = self.source[u]

        def slot(self, part, b):
            return self.target.at[part, b], self.recv.at[part * HALF + b]

        def passing(self, b):
            ref, sem = self.slot(relayed, b)
            return remote(ref, ref, self.forward.at[b], sem, head=beyond)

        def pass_on(self):
            @pl.when(relay)
            def _():
                def step(d):
                    b = (u + d) % HALF
                    landed(self.slot(relayed, b))
                    self.passing(b).start()

                over(0, HALF, step)

        def arrive(self):
            def step(d):
                p = peer(d)

                landed(self.slot(p // HALF, p % HALF))

            over(1, HEADSETS * HALF, step)

        def sent(self):
            self.direct("wait_send")

    gathers = [
        Gather(att_small, small_recv, as_s, as_r, fs_s),
        Gather(att_large, large_recv, al_s, al_r, fl_s),
    ]

    def piece(part, column, start, count):
        rows = pl.ds(pl.multiple_of(part * W + start, 16), count)
        return wout.at[core, rows, 0:VIA_X] if column == 0 else wout.at[core, rows, VIA_X:WIDE]

    def first_rows(column):
        return x * 64 + y * 16 if column == 0 else y * 64 + x * 16

    def wz_copy(i):
        to = (h + 1 + i) % HEADSETS
        ref = piece(h, 0, first_rows(0), 16)
        return remote(ref, ref, wz_s.at[to], wz_r.at[h], head=to)

    def vz_copy(i):
        to = (h + 1 + i) % HEADSETS
        ref = piece(h, 1, first_rows(1), 16)
        return remote(ref, ref, wz_s.at[4 + to], wz_r.at[4 + h], head=to)

    def y_place(i):
        return (y + 1 + i // 3) % 4, (h + 1 + i % 3) % HEADSETS

    def x_place(i):
        return (x + 1 + i // 3) % DPS, (h + 1 + i % 3) % HEADSETS

    def ay_copy(i):
        to, part = y_place(i)
        ref = piece(part, 0, first_rows(0), 16)
        return remote(
            ref, ref, ay_s.at[to * 4 + part], ay_r.at[y * 4 + part], seq=in_half(to * 2 + core)
        )

    def bx_copy(i):
        to, part = x_place(i)
        ref = piece(part, 1, first_rows(1), 16)
        return remote(ref, ref, bx_s.at[to * 4 + part], bx_r.at[x * 4 + part], dp=to)

    def ax_copy(i):
        to, part = x_place(i)
        ref = piece(part, 0, x * 64, 64)
        return remote(ref, ref, ax_s.at[to * 4 + part], ax_r.at[x * 4 + part], dp=to)

    def by_copy(i):
        to, part = y_place(i)
        ref = piece(part, 1, y * 64, 64)
        return remote(
            ref, ref, by_s.at[to * 4 + part], by_r.at[y * 4 + part], seq=in_half(to * 2 + core)
        )

    def wc_copy(i):
        part = (h + 1 + i) % HEADSETS
        ref = wout.at[core, pl.ds(pl.multiple_of(part * W, W), W), :]
        return remote(ref, ref, wc_s.at[part], wc_r.at[part], seq=in_half(u + 1 - 2 * core))

    groups = {
        "mod_a": (1, HEADSETS, mod_a_copy, lambda d: (mod_a.at[(h + d) % HEADSETS], ma_r.at[(h + d) % HEADSETS])),
        "mod_b": (1, HALF, mod_b_copy, lambda d: (mod_b.at[(u + d) % HALF], mb_r.at[(u + d) % HALF])),
        "cache": (1, 16, cache_copy, lambda d: (cache_recv.at[(seq + d) % 16], ca_r.at[(seq + d) % 16])),
        "small_near": (
            1, HALF, small_near_copy, lambda d: (small_near.at[(u + d) % HALF], sn_r.at[(u + d) % HALF]),
        ),
        "small_far": (
            0, HALF, small_far_copy, lambda d: (small_far.at[(u + d) % HALF], sf_r.at[(u + d) % HALF]),
        ),
        "large_near": (
            1, HALF, large_near_copy, lambda d: (large_near.at[(u + d) % HALF], ln_r.at[(u + d) % HALF]),
        ),
        "wz": (
            0, 3, wz_copy,
            lambda i: (piece((h + 1 + i) % HEADSETS, 0, first_rows(0), 16), wz_r.at[(h + 1 + i) % HEADSETS]),
        ),
        "vz": (
            0, 3, vz_copy,
            lambda i: (piece((h + 1 + i) % HEADSETS, 1, first_rows(1), 16), wz_r.at[4 + (h + 1 + i) % HEADSETS]),
        ),
        "ay": (
            0, 9, ay_copy,
            lambda i: (
                piece(y_place(i)[1], 0, x * 64 + y_place(i)[0] * 16, 16),
                ay_r.at[y_place(i)[0] * 4 + y_place(i)[1]],
            ),
        ),
        "bx": (
            0, 9, bx_copy,
            lambda i: (
                piece(x_place(i)[1], 1, y * 64 + x_place(i)[0] * 16, 16),
                bx_r.at[x_place(i)[0] * 4 + x_place(i)[1]],
            ),
        ),
        "ax": (
            0, 9, ax_copy,
            lambda i: (
                piece(x_place(i)[1], 0, x_place(i)[0] * 64, 64), ax_r.at[x_place(i)[0] * 4 + x_place(i)[1]],
            ),
        ),
        "by": (
            0, 9, by_copy,
            lambda i: (
                piece(y_place(i)[1], 1, y_place(i)[0] * 64, 64), by_r.at[y_place(i)[0] * 4 + y_place(i)[1]],
            ),
        ),
        "wc": (
            0, 3, wc_copy,
            lambda i: (
                wout.at[1 - core, pl.ds(pl.multiple_of(((h + 1 + i) % HEADSETS) * W, W), W), :],
                wc_r.at[(h + 1 + i) % HEADSETS],
            ),
        ),
    }

    def over(low, high, action):
        def step(d, c):
            action(d)
            return c

        lax.fori_loop(low, high, step, 0)

    def landed(place):
        slot, sem = place
        remote(slot, slot, ma_s.at[0], sem, head=(h + 1) % HEADSETS).wait_recv()

    def start(name):
        low, high, copy, _ = groups[name]
        over(low, high, lambda d: copy(d).start())

    def arrive(name):
        low, high, _, arrival = groups[name]
        over(low, high, lambda d: landed(arrival(d)))

    def sent(name):
        low, high, copy, _ = groups[name]
        over(low, high, lambda d: copy(d).wait_send())

    partner = [
        remote(position.at[0], far_position, fp_s.at[0], fp_r.at[0], seq=in_other(u)),
        remote(feature_sum, far_features, fp_s.at[1], fp_r.at[1], seq=in_other(u)),
    ]

    loads["labels"].wait()
    loads["table"].wait()
    owned = table.shape[1]
    rows8 = iota((IMG, owned), 0)
    wanted = jnp.zeros((IMG, owned), jnp.int32)
    for b in range(IMG):
        wanted = jnp.where(rows8 == b, labels[b] - h * owned, wanted)
    onehot = flags(wanted == iota((IMG, owned), 1))
    parts = [dot(onehot, table[t]) for t in range(3)] + [jnp.zeros((IMG, W), F32)]
    mod_a[h] = jnp.concatenate(parts, axis=0).astype(BF16)

    group = flags((iota((W, W), 0) >> 6) == (iota((W, W), 1) >> 6))

    def normalize(v):
        high, low = split(v * v)
        return v * lax.rsqrt(dot(high, group) + dot(low, group) + 1e-06)

    loads["cache"].wait()
    r, c = iota((W, W), 0), iota((W, W), 1)
    to_kind = flags(c == ((r >> 5) * 32 + (r & 15) * 2 + ((r >> 4) & 1)))
    moved = dot(to_kind, cache[...].reshape(W, W))
    moved = jnp.where(((r >> 4) & 1) == 0, normalize(moved), moved)
    cache_send[...] = moved.astype(BF16).reshape(IMG, 32, W)
    cache_recv[seq] = cache_send[u]
    loads["position"].wait()
    loads["features"].wait()
    loads["ids"].wait()

    pl.semaphore_wait(barrier, HEADSETS * HALF - 1 + HALF + DPS - 1)
    start("mod_a")
    for copy in partner:
        copy.start()
    loads["out0"].wait()
    loads["out1"].wait()
    start("wz")
    start("vz")

    taps = []
    for n, row in enumerate((seq, (seq + HALF) % 16)):
        place = 26 * row - 3 + 3 * ((16 - row) // 16)
        lower = place // 32
        upper = lower + 1 - lower // (S13 - 1)
        taps.append((place % 32).astype(F32) * (1.0 / 32.0))
        for t, source in enumerate((ids[lower], ids[upper])):
            for j in range(S13):
                id_lanes[2 * n + t, j] = jnp.broadcast_to(source[:, j : j + 1], (IMG, 128))
    loads["codebook"].wait()

    def look(c, total):
        start_at = pl.multiple_of(c * SPAN, SPAN)
        columns = []
        for q in range(SPAN // 128):
            entry = iota((IMG, 128), 1) + (c * SPAN + q * 128)
            hits = []
            for n in range(2):
                for j in range(S13):
                    hits.append(
                        jnp.where(id_lanes[2 * n, j] == entry, 1.0 - taps[n], 0.0)
                        + jnp.where(id_lanes[2 * n + 1, j] == entry, taps[n], 0.0)
                    )
            columns.append(jnp.concatenate(hits, axis=0).astype(BF16))
        both = jnp.concatenate(split(codebook[:, pl.ds(start_at, SPAN)]), axis=0)
        return total + dot_nt(jnp.concatenate(columns, axis=1), both)

    looked = lax.fori_loop(0, codebook.shape[1] // SPAN, look, jnp.zeros((2 * SMALL, 64), F32))
    looked = looked[:, 0:32] + looked[:, 32:64]

    arrive("mod_a")
    total = mod_a[0].astype(F32)
    for part in range(1, HEADSETS):
        total = total + mod_a[part].astype(F32)
    mod_b[u] = total.astype(BF16)
    start("mod_b")
    start("cache")

    loads["thirteen"].wait()
    first = 2 * LARGE
    for i in range(SMALL // 16):
        xhat[first + 16 * i : first + 16 * i + 16, :] = layer_norm(thirteen[16 * i : 16 * i + 16, :].astype(F32))
    xhat[ROWS - 16 : ROWS - 8, :] = layer_norm(thirteen[SMALL - 8 : SMALL, :].astype(F32))
    xhat[ROWS - 8 : ROWS, :] = jnp.zeros((8, D), F32)
    loads["embed"].wait()
    loads["bias"].wait()
    embed_high, embed_low = split(embed[...])
    embed_parts = jnp.concatenate([embed_high, embed_low, embed_high], axis=0)
    bias_row = bias[...].reshape(1, D)

    def embedded(first, source, rows, table_rows):
        features = []
        for s in range(S16):
            at = max(26 * s - 3, 0)
            low = at // 32
            up = min(low + 1, S13 - 1)
            frac = (at % 32) / 32.0
            features.append(
                source[:, s * 32 : (s + 1) * 32]
                + rows[low * IMG : (low + 1) * IMG] * (1.0 - frac)
                + rows[up * IMG : (up + 1) * IMG] * frac
            )
        high, low = split(jnp.concatenate(features, axis=0))
        xhat[first : first + LARGE, :] = dot(jnp.concatenate([high, high, low], axis=1), embed_parts)
        for i in range(S16 // 2):
            pair = table_rows[2 * i : 2 * i + 2, :].astype(F32)
            pair = jnp.concatenate([jnp.broadcast_to(pair[k : k + 1], (IMG, D)) for k in range(2)], axis=0)
            at = first + 16 * i
            row = xhat[at : at + 16, :] + bias_row + pair
            xhat[at : at + 16, :] = layer_norm(row.astype(BF16).astype(F32))

    embedded(0, feature_sum[:, 0, :], looked[0:SMALL], position[0])
    for copy in partner:
        copy.wait_recv()
    embedded(LARGE, far_features[:, 0, :], looked[SMALL : 2 * SMALL], far_position[...])

    arrive("wz")
    arrive("vz")
    start("ay")
    start("bx")
    arrive("mod_b")
    for c in range(HALF):
        chunk = mod_b[c].astype(F32)
        if c == HALF - 1:
            chunk = chunk[:, 128:]
        width = chunk.shape[1]
        mod[0, :, c * W : c * W + width] = chunk[0:8]
        mod[1, :, c * W : c * W + width] = 1.0 + chunk[8:16]
        mod[2, :, c * W : c * W + width] = chunk[16:24]

    def modulate(i):
        at = pl.multiple_of(i * 16, 16)
        rows = xhat[pl.ds(at, 16), :].reshape(2, IMG, D)
        rows = rows * mod[1][None] + mod[0][None]
        xmod[pl.ds(at, 16), :] = rows.reshape(16, D).astype(BF16)

    loads["scale"].wait()
    lane_head = iota((1, W), 1) >> 6
    scales = jnp.zeros((1, W), F32)
    for k in range(4):
        scales = jnp.where(lane_head == k, head_scale[k], scales)

    over(0, ROWS // 16, modulate)
    loads["qkv"].wait()
    r, c = iota((LARGE, PADDED), 0), iota((LARGE, PADDED), 1)
    small_to_image = flags(((r & 15) < S13) & (c == (r & 15) * IMG + (r >> 4)))
    r, c = iota((LARGE, LARGE), 0), iota((LARGE, LARGE), 1)
    large_to_image = flags(c == (r & 15) * IMG + (r >> 4))

    def moved_small(rows):
        return dot(small_to_image, rows).astype(BF16).reshape(IMG, TOK, W)

    def moved_large(rows):
        return dot(large_to_image, rows).astype(BF16).reshape(IMG, TOK, W)

    keys = normalize(dot(xmod[...], qkv[1])).astype(BF16)
    small_send[:, TOK : 2 * TOK, :] = moved_small(keys[2 * LARGE :])
    values = dot(xmod[...], qkv[2]).astype(BF16)
    small_send[:, 2 * TOK : 3 * TOK, :] = moved_small(values[2 * LARGE :])
    start("small_far")
    for slot, rows in ((1, keys[0:LARGE]), (2, values[0:LARGE]), (3, keys[LARGE : 2 * LARGE]), (4, values[LARGE : 2 * LARGE])):
        large_send[:, slot * TOK : (slot + 1) * TOK, :] = moved_large(rows)
    small_queries = normalize(dot(xmod[2 * LARGE :, :], qkv[0])) * scales
    small_send[:, 0:TOK, :] = moved_small(small_queries.astype(BF16))
    start("small_near")
    small_near[u] = small_send[u]
    large_queries = normalize(dot(xmod[0:LARGE, :], qkv[0])) * scales
    large_send[:, 0:TOK, :] = moved_large(large_queries.astype(BF16))
    start("large_near")
    large_near[u] = large_send[u]
    arrive("ay")
    arrive("bx")
    start("ax")
    start("by")

    lanes = iota((W, W), 1) >> 6
    key = iota((W, W), 0)

    def by_head(rows):
        return [
            jnp.where(lanes[0:LARGE] == k, rows, jnp.zeros_like(rows)) for k in range(4)
        ]

    def offer(index, values, valid):
        for k in range(4):
            row = (index * 4 + k) * W
            use = lanes == k
            if valid is not None:
                use = use & valid
            vext[row : row + W, 0:W] = jnp.where(use, values, jnp.zeros_like(values))
            vext[row : row + W, W : 2 * W] = flags(use)

    def weigh(index, queries, keys):
        for k in range(4):
            column = (index * 4 + k) * W
            weights[:, column : column + W] = jnp.exp(dot_nt(queries[k], keys)).astype(BF16)

    def attend(queries, keys, out):
        for index, block in enumerate(keys):
            weigh(index, queries, block)
        used = len(keys) * 4 * W
        sums = dot(weights[:, 0:used], vext[0:used, :])
        out[...] = (sums[:, 0:W] / sums[:, W : 2 * W]).astype(BF16).reshape(HALF, TOK, W)

    arrive("cache")
    cache_keys = cache_recv[:, 0:16, :].reshape(W, W)
    offer(0, cache_recv[:, 16:32, :].reshape(W, W), key < W - 1)
    arrive("small_near")
    arrive("small_far")
    small_keys = jnp.concatenate(
        [small_near[:, TOK : 2 * TOK, :].reshape(LARGE, W), small_far[:, 0:TOK, :].reshape(LARGE, W)], axis=0
    )
    small_values = jnp.concatenate(
        [small_near[:, 2 * TOK : 3 * TOK, :].reshape(LARGE, W), small_far[:, TOK : 2 * TOK, :].reshape(LARGE, W)],
        axis=0,
    )
    map_row = (key >> 4) + HALF * zh * jnp.where(key < LARGE, 1, -1)
    offer(1, small_values, ((key & 15) < S13) & (map_row < S13))
    attend(by_head(small_near[:, 0:TOK, :].reshape(LARGE, W)), [cache_keys, small_keys], att_small)
    gathers[0].start()

    arrive("large_near")
    large_keys = jnp.concatenate(
        [large_near[:, k * TOK : (k + 1) * TOK, :].reshape(LARGE, W) for k in (1, 3)], axis=0
    )
    large_values = jnp.concatenate(
        [large_near[:, k * TOK : (k + 1) * TOK, :].reshape(LARGE, W) for k in (2, 4)], axis=0
    )
    offer(2, large_values, None)
    attend(
        by_head(large_near[:, 0:TOK, :].reshape(LARGE, W)), [cache_keys, small_keys, large_keys], att_large
    )
    gathers[1].start()
    arrive("ax")
    arrive("by")
    start("wc")

    r, c = iota((PADDED, LARGE), 0), iota((PADDED, LARGE), 1)
    to_row = flags(c == (r & 7) * TOK + (r >> 3))
    kept = seq < S13

    def project_small(side):
        def step(i):
            inner = pl.multiple_of(i * W, W)
            outer = pl.ds(pl.multiple_of(side * SECOND + inner, 128), W)
            branch = dot(small_all[...], wout[side, :, pl.ds(inner, W)])
            gate = mod[2, :, outer]
            for j in range(S13):
                rows = gate * branch[j * IMG : (j + 1) * IMG]
                o13[j, :, outer] = jnp.where(kept, rows, jnp.zeros_like(rows)).astype(BF16)

        over(0, WIDE // W, step)

    def project_large(side):
        def step(i):
            inner = pl.multiple_of(i * W, W)
            outer = pl.ds(pl.multiple_of(side * SECOND + inner, 128), W)
            branch = dot(large_all[...], wout[side, :, pl.ds(inner, W)])
            gate = mod[2, :, outer]
            for b in range(IMG):
                o16[b, :, outer] = (gate[b : b + 1] * branch[b * S16 : (b + 1) * S16]).astype(BF16)

        over(0, WIDE // W, step)

    gathers[0].arrive()
    for k in range(HEADSETS):
        small_all[:, k * W : (k + 1) * W] = dot(to_row, small_recv[k].reshape(LARGE, W)).astype(BF16)
    project_small(core)
    gathers[1].arrive()
    for k in range(HEADSETS):
        large_all[:, k * W : (k + 1) * W] = large_recv[k].reshape(LARGE, W)
    project_large(core)
    arrive("wc")
    project_small(1 - core)
    project_large(1 - core)

    for copy in partner:
        copy.wait_send()
    for name in groups:
        sent(name)
    for gather in gathers:
        gather.sent()


def hand_on(a_ref, b_ref, a_out, b_out, sem):
    copies = [
        pltpu.make_async_copy(source.at[i : i + n], target.at[i : i + n], sem.at[k])
        for k, (source, target, i, n) in enumerate(
            ((a_ref, a_out, 0, 7), (a_ref, a_out, 7, 6), (b_ref, b_out, 0, 4), (b_ref, b_out, 4, 4))
        )
    ]
    for copy in copies:
        copy.start()
    for copy in copies:
        copy.wait()


def body(
    map_thirteen, kv_cache, class_labels, class_table, sampled_ids, codebook, feature_sum,
    embed_weight, embed_bias, position_table, qkv_weight, out_weight, head_scale,
):
    owned = class_table.shape[0]
    vocabulary = codebook.shape[0]
    vmem = pl.BlockSpec(memory_space=pltpu.VMEM)
    anywhere = pl.BlockSpec(memory_space=pl.ANY)
    dma = pltpu.SemaphoreType.DMA
    o13, o16 = pl.pallas_call(
        kernel,
        out_shape=(
            jax.ShapeDtypeStruct((S13, IMG, D), BF16),
            jax.ShapeDtypeStruct((IMG, S16, D), BF16),
        ),
        in_specs=[anywhere] * 13,
        out_specs=(vmem, vmem),
        scratch_shapes=[
            pltpu.SMEM((IMG,), jnp.int32),
            pltpu.SMEM(head_scale.shape, F32),
            pltpu.VMEM((S13, IMG, S13), jnp.int32),
            pltpu.VMEM((IMG, 16, 2, W), BF16),
            pltpu.VMEM((IMG, 1, S16 * 32), F32),
            pltpu.VMEM((D,), F32),
            pltpu.VMEM((1, S16, D), BF16),
            pltpu.VMEM((SMALL, D), BF16),
            pltpu.VMEM((3, owned, W), BF16),
            pltpu.VMEM((32, vocabulary), F32),
            pltpu.VMEM((32, D), F32),
            pltpu.VMEM((3, D, W), BF16),
            pltpu.VMEM((2, HEADSETS * W, WIDE), BF16),
            pltpu.VMEM((IMG, 32, W), BF16),
            pltpu.VMEM((16, 32, W), BF16),
            pltpu.VMEM((HEADSETS, 32, W), BF16),
            pltpu.VMEM((HALF, 32, W), BF16),
            pltpu.VMEM((3, IMG, D), F32),
            pltpu.VMEM((S16, D), BF16),
            pltpu.VMEM((IMG, 1, S16 * 32), F32),
            pltpu.VMEM((4, S13, IMG, 128), jnp.int32),
            pltpu.VMEM((ROWS, D), F32),
            pltpu.VMEM((ROWS, D), BF16),
            pltpu.VMEM((IMG, 3 * TOK, W), BF16),
            pltpu.VMEM((HALF, 3 * TOK, W), BF16),
            pltpu.VMEM((HALF, 2 * TOK, W), BF16),
            pltpu.VMEM((IMG, 5 * TOK, W), BF16),
            pltpu.VMEM((HALF, 5 * TOK, W), BF16),
            pltpu.VMEM((LARGE, 12 * W), BF16),
            pltpu.VMEM((12 * W, 2 * W), BF16),
            pltpu.VMEM((HALF, TOK, W), BF16),
            pltpu.VMEM((HALF, TOK, W), BF16),
            pltpu.VMEM((HEADSETS, HALF, TOK, W), BF16),
            pltpu.VMEM((HEADSETS, HALF, TOK, W), BF16),
            pltpu.VMEM((PADDED, HEADSETS * W), BF16),
            pltpu.VMEM((LARGE, HEADSETS * W), BF16),
            dma((14,)),
        ]
        + [dma((n,)) for n in (
            4, 4, 8, 8, 2, 2, 16, 16, 8, 8, 8, 8, 8, 8, 32, 32, 32, 32, 8, 8, 8, 8, 16, 16, 16, 16, 16, 16, 16, 16, 4, 4
        )],
        compiler_params=pltpu.CompilerParams(
            collective_id=0, has_side_effects=True, vmem_limit_bytes=VMEM_LIMIT
        ),
        cost_estimate=pl.CostEstimate(flops=3_000_000_000, bytes_accessed=12_000_000, transcendentals=1_000_000),
    )(
        class_labels,
        head_scale,
        sampled_ids.transpose(1, 0, 2),
        kv_cache,
        feature_sum,
        embed_bias,
        position_table,
        map_thirteen.reshape(IMG, S13, D).transpose(1, 0, 2).reshape(SMALL, D),
        class_table.transpose(1, 0, 2),
        codebook.T,
        embed_weight,
        qkv_weight.transpose(1, 0, 2),
        out_weight,
    )
    o13, o16 = pl.pallas_call(
        hand_on,
        out_shape=(
            jax.ShapeDtypeStruct((S13, IMG, D), BF16),
            jax.ShapeDtypeStruct((IMG, S16, D), BF16),
        ),
        in_specs=[vmem] * 2,
        out_specs=(anywhere, anywhere),
        scratch_shapes=[dma((4,))],
        cost_estimate=pl.CostEstimate(flops=0, bytes_accessed=1_800_000, transcendentals=0),
    )(o13, o16)
    return o13.transpose(1, 0, 2)[:, None], o16[:, None]


def solution(mesh):
    placed = (
        P("dp", "seq", None, None),
        P("dp", "seq", None, "head"),
        P("dp"),
        P("head", None, None),
        P("dp", None, None),
        P(),
        P("dp", "seq", None),
        P(),
        P(),
        P("seq", None, None),
        P(None, None, "head"),
        P("head", None),
        P("head"),
    )
    return jax.shard_map(
        body,
        mesh=mesh,
        in_specs=placed,
        out_specs=(P("dp", "seq", None, None), P("dp", "seq", None, None)),
        check_vma=False,
    )
```

```python
import functools

import jax
import jax.numpy as jnp
from jax import lax
from jax.experimental import pallas as pl
from jax.experimental.pallas import tpu as pltpu
from jax.sharding import PartitionSpec as P

MESH = pl.DeviceIdType.MESH
S13 = 13
S16 = 16
D = 1920
W = 256
IMG = 8
HALF = 8
HEADSETS = 4
DPS = 4
TOK = 16
LARGE = IMG * S16
SMALL = IMG * S13
PADDED = SMALL + IMG
ROWS = 2 * LARGE + PADDED
SPAN = 512
PART = 512
VIA_X = 768
WIDE = 1024
SECOND = D - WIDE
F32 = jnp.float32
BF16 = jnp.bfloat16
VMEM_LIMIT = 58 * 1024 * 1024


def dot(a, b):
    return jnp.dot(a, b, preferred_element_type=F32)


def dot_nt(a, b):
    return lax.dot_general(a, b, (((1,), (1,)), ((), ())), preferred_element_type=F32)


def iota(shape, axis):
    return lax.broadcasted_iota(jnp.int32, shape, axis)


def flags(condition):
    return jnp.where(condition, 1.0, 0.0).astype(BF16)


def split(x):
    high = x.astype(BF16)
    return high, (x - high.astype(F32)).astype(BF16)


def layer_norm(x):
    centred = x - jnp.mean(x, axis=-1, keepdims=True)
    variance = jnp.mean(centred * centred, axis=-1, keepdims=True)
    return centred * lax.rsqrt(variance + 1e-06)


def remote(src, dst, send, recv, **device):
    return pltpu.make_async_remote_copy(
        src_ref=src, dst_ref=dst, send_sem=send, recv_sem=recv, device_id=device, device_id_type=MESH
    )


def kernel(
    labels_hbm, scale_hbm, ids_hbm, cache_hbm, features_hbm, bias_hbm, position_hbm,
    thirteen_hbm, table_hbm, codebook_hbm, embed_hbm, qkv_hbm, out_hbm,
    o13, o16,
    labels, head_scale, ids, cache, feature_sum, bias, position,
    thirteen, table, codebook, embed, qkv, wout,
    cache_send, cache_recv, mod_a, mod_b, mod, far_position, far_features, id_lanes, xhat, xmod,
    small_send, small_near, small_far, large_send, large_near,
    weights, vext, att_small, att_large, small_recv, large_recv, small_all, large_all, both_all,
    local_sem,
    ma_s, ma_r, mb_s, mb_r, fp_s, fp_r, sp_s, sp_r, ca_s, ca_r, sn_s, sn_r, sf_s, sf_r, ln_s, ln_r,
    as_s, as_r, al_s, al_r, fs_s, fl_s,
    wz_s, wz_r, ay_s, ay_r, bx_s, bx_r, ax_s, ax_r, by_s, by_r, wc_s, wc_r,
):
    x = lax.axis_index("dp")
    seq = lax.axis_index("seq")
    h = lax.axis_index("head")
    zh, u = seq // HALF, seq % HALF
    y, core = u // 2, u % 2
    me = h * HALF + u

    def in_half(place):
        return zh * HALF + place

    def in_other(place):
        return (1 - zh) * HALF + place

    barrier = pltpu.get_barrier_semaphore()

    def greet_half(d, c):
        p = (me + d) % (HEADSETS * HALF)
        pl.semaphore_signal(
            barrier, inc=1, device_id={"seq": in_half(p % HALF), "head": p // HALF}, device_id_type=MESH
        )
        return c

    def greet_other(d, c):
        pl.semaphore_signal(
            barrier, inc=1, device_id={"seq": in_other((u + d) % HALF)}, device_id_type=MESH
        )
        return c

    def greet_dp(d, c):
        pl.semaphore_signal(barrier, inc=1, device_id={"dp": (x + d) % DPS}, device_id_type=MESH)
        return c

    lax.fori_loop(0, HALF, greet_other, 0)
    lax.fori_loop(1, HEADSETS * HALF, greet_half, 0)
    lax.fori_loop(1, DPS, greet_dp, 0)

    col0 = pl.multiple_of(u * W - (u // 7) * 128, 128)
    loads = [
        (labels_hbm, labels),
        (table_hbm.at[:, :, pl.ds(col0, W)], table),
        (cache_hbm, cache),
        (position_hbm, position),
        (features_hbm, feature_sum),
        (ids_hbm, ids),
        (codebook_hbm, codebook),
        (out_hbm.at[:, pl.ds(0, WIDE)], wout.at[0, pl.ds(pl.multiple_of(h * W, W), W), :]),
        (out_hbm.at[:, pl.ds(SECOND, WIDE)], wout.at[1, pl.ds(pl.multiple_of(h * W, W), W), :]),
        (thirteen_hbm, thirteen),
        (embed_hbm, embed),
        (bias_hbm, bias),
        (scale_hbm, head_scale),
        (qkv_hbm, qkv),
    ]
    names = (
        "labels", "table", "cache", "position", "features", "ids", "codebook", "out0", "out1", "thirteen",
        "embed", "bias", "scale", "qkv",
    )
    loads = {
        name: pltpu.make_async_copy(a, b, local_sem.at[i]) for i, (name, (a, b)) in enumerate(zip(names, loads))
    }
    for load in loads.values():
        load.start()

    def mod_a_copy(d):
        to = (h + d) % HEADSETS
        return remote(mod_a.at[h], mod_a.at[h], ma_s.at[to], ma_r.at[h], head=to)

    def mod_b_copy(d):
        to = (u + d) % HALF
        return remote(mod_b.at[u], mod_b.at[u], mb_s.at[to], mb_r.at[u], seq=in_half(to))

    def spread_copy(d):
        to = (x + d) % DPS
        return remote(far_position.at[x], far_position.at[x], sp_s.at[to], sp_r.at[x], dp=to)

    def cache_copy(d):
        to = (seq + d) % 16
        return remote(cache_send.at[to % HALF], cache_recv.at[seq], ca_s.at[to], ca_r.at[seq], seq=to)

    def small_near_copy(d):
        to = (u + d) % HALF
        return remote(small_send.at[to], small_near.at[u], sn_s.at[to], sn_r.at[u], seq=in_half(to))

    def small_far_copy(d):
        to = (u + d) % HALF
        return remote(
            small_send.at[to, pl.ds(TOK, 2 * TOK), :], small_far.at[u], sf_s.at[to], sf_r.at[u],
            seq=in_other(to),
        )

    def large_near_copy(d):
        to = (u + d) % HALF
        return remote(large_send.at[to], large_near.at[u], ln_s.at[to], ln_r.at[u], seq=in_half(to))

    def peer(d):
        return (me + d) % (HEADSETS * HALF)

    relay = (h % 3) > 0
    relayed, beyond = 3 * (2 - h), 3 * (h - 1)

    class Gather:
        def __init__(self, source, target, send, recv, forward):
            self.source, self.target, self.send, self.recv, self.forward = source, target, send, recv, forward

        def copy(self, p):
            return remote(
                self.source.at[p % HALF], self.target.at[h, u], self.send.at[p], self.recv.at[me],
                seq=in_half(p % HALF), head=p // HALF,
            )

        def direct(self, action):
            def step(d):
                p = peer(d)

                getattr(self.copy(p), action)()

            over(1, HEADSETS * HALF, step)

        def start(self):
            self.direct("start")
            self.target[h, u] = self.source[u]

        def slot(self, part, b):
            return self.target.at[part, b], self.recv.at[part * HALF + b]

        def passing(self, b):
            ref, sem = self.slot(relayed, b)
            return remote(ref, ref, self.forward.at[b], sem, head=beyond)

        def pass_on(self):
            @pl.when(relay)
            def _():
                def step(d):
                    b = (u + d) % HALF
                    landed(self.slot(relayed, b))
                    self.passing(b).start()

                over(0, HALF, step)

        def arrive(self):
            def step(d):
                p = peer(d)

                landed(self.slot(p // HALF, p % HALF))

            over(1, HEADSETS * HALF, step)

        def sent(self):
            self.direct("wait_send")

    gathers = [
        Gather(att_small, small_recv, as_s, as_r, fs_s),
        Gather(att_large, large_recv, al_s, al_r, fl_s),
    ]

    def piece(part, column, start, count):
        rows = pl.ds(pl.multiple_of(part * W + start, 16), count)
        return wout.at[core, rows, 0:VIA_X] if column == 0 else wout.at[core, rows, VIA_X:WIDE]

    def first_rows(column):
        return x * 64 + y * 16 if column == 0 else y * 64 + x * 16

    def wz_copy(i):
        to = (h + 1 + i) % HEADSETS
        ref = piece(h, 0, first_rows(0), 16)
        return remote(ref, ref, wz_s.at[to], wz_r.at[h], head=to)

    def vz_copy(i):
        to = (h + 1 + i) % HEADSETS
        ref = piece(h, 1, first_rows(1), 16)
        return remote(ref, ref, wz_s.at[4 + to], wz_r.at[4 + h], head=to)

    def y_place(i):
        return (y + 1 + i // 3) % 4, (h + 1 + i % 3) % HEADSETS

    def x_place(i):
        return (x + 1 + i // 3) % DPS, (h + 1 + i % 3) % HEADSETS

    def ay_copy(i):
        to, part = y_place(i)
        ref = piece(part, 0, first_rows(0), 16)
        return remote(
            ref, ref, ay_s.at[to * 4 + part], ay_r.at[y * 4 + part], seq=in_half(to * 2 + core)
        )

    def bx_copy(i):
        to, part = x_place(i)
        ref = piece(part, 1, first_rows(1), 16)
        return remote(ref, ref, bx_s.at[to * 4 + part], bx_r.at[x * 4 + part], dp=to)

    def ax_copy(i):
        to, part = x_place(i)
        ref = piece(part, 0, x * 64, 64)
        return remote(ref, ref, ax_s.at[to * 4 + part], ax_r.at[x * 4 + part], dp=to)

    def by_copy(i):
        to, part = y_place(i)
        ref = piece(part, 1, y * 64, 64)
        return remote(
            ref, ref, by_s.at[to * 4 + part], by_r.at[y * 4 + part], seq=in_half(to * 2 + core)
        )

    def wc_copy(i):
        part = (h + 1 + i) % HEADSETS
        ref = wout.at[core, pl.ds(pl.multiple_of(part * W, W), W), :]
        return remote(ref, ref, wc_s.at[part], wc_r.at[part], seq=in_half(u + 1 - 2 * core))

    groups = {
        "mod_a": (1, HEADSETS, mod_a_copy, lambda d: (mod_a.at[(h + d) % HEADSETS], ma_r.at[(h + d) % HEADSETS])),
        "mod_b": (1, HALF, mod_b_copy, lambda d: (mod_b.at[(u + d) % HALF], mb_r.at[(u + d) % HALF])),
        "spread": (1, DPS, spread_copy, lambda d: (far_position.at[(x + d) % DPS], sp_r.at[(x + d) % DPS])),
        "cache": (1, 16, cache_copy, lambda d: (cache_recv.at[(seq + d) % 16], ca_r.at[(seq + d) % 16])),
        "small_near": (
            1, HALF, small_near_copy, lambda d: (small_near.at[(u + d) % HALF], sn_r.at[(u + d) % HALF]),
        ),
        "small_far": (
            0, HALF, small_far_copy, lambda d: (small_far.at[(u + d) % HALF], sf_r.at[(u + d) % HALF]),
        ),
        "large_near": (
            1, HALF, large_near_copy, lambda d: (large_near.at[(u + d) % HALF], ln_r.at[(u + d) % HALF]),
        ),
        "wz": (
            0, 3, wz_copy,
            lambda i: (piece((h + 1 + i) % HEADSETS, 0, first_rows(0), 16), wz_r.at[(h + 1 + i) % HEADSETS]),
        ),
        "vz": (
            0, 3, vz_copy,
            lambda i: (piece((h + 1 + i) % HEADSETS, 1, first_rows(1), 16), wz_r.at[4 + (h + 1 + i) % HEADSETS]),
        ),
        "ay": (
            0, 9, ay_copy,
            lambda i: (
                piece(y_place(i)[1], 0, x * 64 + y_place(i)[0] * 16, 16),
                ay_r.at[y_place(i)[0] * 4 + y_place(i)[1]],
            ),
        ),
        "bx": (
            0, 9, bx_copy,
            lambda i: (
                piece(x_place(i)[1], 1, y * 64 + x_place(i)[0] * 16, 16),
                bx_r.at[x_place(i)[0] * 4 + x_place(i)[1]],
            ),
        ),
        "ax": (
            0, 9, ax_copy,
            lambda i: (
                piece(x_place(i)[1], 0, x_place(i)[0] * 64, 64), ax_r.at[x_place(i)[0] * 4 + x_place(i)[1]],
            ),
        ),
        "by": (
            0, 9, by_copy,
            lambda i: (
                piece(y_place(i)[1], 1, y_place(i)[0] * 64, 64), by_r.at[y_place(i)[0] * 4 + y_place(i)[1]],
            ),
        ),
        "wc": (
            0, 3, wc_copy,
            lambda i: (
                wout.at[1 - core, pl.ds(pl.multiple_of(((h + 1 + i) % HEADSETS) * W, W), W), :],
                wc_r.at[(h + 1 + i) % HEADSETS],
            ),
        ),
    }

    def over(low, high, action):
        def step(d, c):
            action(d)
            return c

        lax.fori_loop(low, high, step, 0)

    def landed(place):
        slot, sem = place
        remote(slot, slot, ma_s.at[0], sem, head=(h + 1) % HEADSETS).wait_recv()

    def start(name):
        low, high, copy, _ = groups[name]
        over(low, high, lambda d: copy(d).start())

    def arrive(name):
        low, high, _, arrival = groups[name]
        over(low, high, lambda d: landed(arrival(d)))

    def sent(name):
        low, high, copy, _ = groups[name]
        over(low, high, lambda d: copy(d).wait_send())

    partner = [
        remote(
            position.at[0, :, pl.ds(pl.multiple_of(x * PART - (x // 3) * 128, 128), PART)], far_position.at[x],
            fp_s.at[0], fp_r.at[0], seq=in_other(u),
        ),
        remote(feature_sum, far_features, fp_s.at[1], fp_r.at[1], seq=in_other(u)),
    ]

    loads["labels"].wait()
    loads["table"].wait()
    owned = table.shape[1]
    rows8 = iota((IMG, owned), 0)
    wanted = jnp.zeros((IMG, owned), jnp.int32)
    for b in range(IMG):
        wanted = jnp.where(rows8 == b, labels[b] - h * owned, wanted)
    onehot = flags(wanted == iota((IMG, owned), 1))
    parts = [dot(onehot, table[t]) for t in range(3)] + [jnp.zeros((IMG, W), F32)]
    mod_a[h] = jnp.concatenate(parts, axis=0).astype(BF16)

    group = flags((iota((W, W), 0) >> 6) == (iota((W, W), 1) >> 6))

    def normalize(v):
        high, low = split(v * v)
        return v * lax.rsqrt(dot(high, group) + dot(low, group) + 1e-06)

    loads["cache"].wait()
    r, c = iota((W, W), 0), iota((W, W), 1)
    to_kind = flags(c == ((r >> 5) * 32 + (r & 15) * 2 + ((r >> 4) & 1)))
    moved = dot(to_kind, cache[...].reshape(W, W))
    moved = jnp.where(((r >> 4) & 1) == 0, normalize(moved), moved)
    cache_send[...] = moved.astype(BF16).reshape(IMG, 32, W)
    cache_recv[seq] = cache_send[u]
    loads["position"].wait()
    loads["features"].wait()
    loads["ids"].wait()

    pl.semaphore_wait(barrier, HEADSETS * HALF - 1 + HALF + DPS - 1)
    start("mod_a")
    loads["out0"].wait()
    loads["out1"].wait()
    start("wz")
    start("vz")
    for copy in partner:
        copy.start()

    taps = []
    for n, row in enumerate((seq, (seq + HALF) % 16)):
        place = 26 * row - 3 + 3 * ((16 - row) // 16)
        lower = place // 32
        upper = lower + 1 - lower // (S13 - 1)
        taps.append((place % 32).astype(F32) * (1.0 / 32.0))
        for t, source in enumerate((ids[lower], ids[upper])):
            for j in range(S13):
                id_lanes[2 * n + t, j] = jnp.broadcast_to(source[:, j : j + 1], (IMG, 128))
    loads["codebook"].wait()

    def look(c, total):
        start_at = pl.multiple_of(c * SPAN, SPAN)
        columns = []
        for q in range(SPAN // 128):
            entry = iota((IMG, 128), 1) + (c * SPAN + q * 128)
            hits = []
            for n in range(2):
                for j in range(S13):
                    hits.append(
                        jnp.where(id_lanes[2 * n, j] == entry, 1.0 - taps[n], 0.0)
                        + jnp.where(id_lanes[2 * n + 1, j] == entry, taps[n], 0.0)
                    )
            columns.append(jnp.concatenate(hits, axis=0).astype(BF16))
        both = jnp.concatenate(split(codebook[:, pl.ds(start_at, SPAN)]), axis=0)
        return total + dot_nt(jnp.concatenate(columns, axis=1), both)

    looked = lax.fori_loop(0, codebook.shape[1] // SPAN, look, jnp.zeros((2 * SMALL, 64), F32))
    looked = looked[:, 0:32] + looked[:, 32:64]

    arrive("mod_a")
    total = mod_a[0].astype(F32)
    for part in range(1, HEADSETS):
        total = total + mod_a[part].astype(F32)
    mod_b[u] = total.astype(BF16)
    start("mod_b")
    start("cache")

    loads["thirteen"].wait()
    first = 2 * LARGE
    for i in range(SMALL // 16):
        xhat[first + 16 * i : first + 16 * i + 16, :] = layer_norm(thirteen[16 * i : 16 * i + 16, :].astype(F32))
    xhat[ROWS - 16 : ROWS - 8, :] = layer_norm(thirteen[SMALL - 8 : SMALL, :].astype(F32))
    xhat[ROWS - 8 : ROWS, :] = jnp.zeros((8, D), F32)
    loads["embed"].wait()
    loads["bias"].wait()
    embed_high, embed_low = split(embed[...])
    embed_parts = jnp.concatenate([embed_high, embed_low, embed_high], axis=0)
    bias_row = bias[...].reshape(1, D)

    def embedded(first, source, rows, table_rows):
        features = []
        for s in range(S16):
            at = max(26 * s - 3, 0)
            low = at // 32
            up = min(low + 1, S13 - 1)
            frac = (at % 32) / 32.0
            features.append(
                source[:, s * 32 : (s + 1) * 32]
                + rows[low * IMG : (low + 1) * IMG] * (1.0 - frac)
                + rows[up * IMG : (up + 1) * IMG] * frac
            )
        high, low = split(jnp.concatenate(features, axis=0))
        xhat[first : first + LARGE, :] = dot(jnp.concatenate([high, high, low], axis=1), embed_parts)
        for i in range(S16 // 2):
            pair = table_rows[2 * i : 2 * i + 2, :].astype(F32)
            pair = jnp.concatenate([jnp.broadcast_to(pair[k : k + 1], (IMG, D)) for k in range(2)], axis=0)
            at = first + 16 * i
            row = xhat[at : at + 16, :] + bias_row + pair
            xhat[at : at + 16, :] = layer_norm(row.astype(BF16).astype(F32))

    partner[0].wait_recv()
    start("spread")
    embedded(0, feature_sum[:, 0, :], looked[0:SMALL], position[0])
    arrive("spread")
    partner[1].wait_recv()
    far_rows = [far_position[k] for k in range(DPS)]
    far_rows[DPS - 1] = far_rows[DPS - 1][:, DPS * PART - D :]
    embedded(LARGE, far_features[:, 0, :], looked[SMALL : 2 * SMALL], jnp.concatenate(far_rows, axis=1))

    arrive("wz")
    arrive("vz")
    start("ay")
    start("bx")
    arrive("mod_b")
    for c in range(HALF):
        chunk = mod_b[c].astype(F32)
        if c == HALF - 1:
            chunk = chunk[:, 128:]
        width = chunk.shape[1]
        mod[0, :, c * W : c * W + width] = chunk[0:8]
        mod[1, :, c * W : c * W + width] = 1.0 + chunk[8:16]
        mod[2, :, c * W : c * W + width] = chunk[16:24]

    def modulate(i):
        at = pl.multiple_of(i * 16, 16)
        rows = xhat[pl.ds(at, 16), :].reshape(2, IMG, D)
        rows = rows * mod[1][None] + mod[0][None]
        xmod[pl.ds(at, 16), :] = rows.reshape(16, D).astype(BF16)

    loads["scale"].wait()
    lane_head = iota((1, W), 1) >> 6
    scales = jnp.zeros((1, W), F32)
    for k in range(4):
        scales = jnp.where(lane_head == k, head_scale[k], scales)

    over(0, ROWS // 16, modulate)
    loads["qkv"].wait()
    r, c = iota((LARGE, PADDED), 0), iota((LARGE, PADDED), 1)
    small_to_image = flags(((r & 15) < S13) & (c == (r & 15) * IMG + (r >> 4)))
    r, c = iota((LARGE, LARGE), 0), iota((LARGE, LARGE), 1)
    large_to_image = flags(c == (r & 15) * IMG + (r >> 4))

    def moved_small(rows):
        return dot(small_to_image, rows).astype(BF16).reshape(IMG, TOK, W)

    def moved_large(rows):
        return dot(large_to_image, rows).astype(BF16).reshape(IMG, TOK, W)

    keys = normalize(dot(xmod[...], qkv[1])).astype(BF16)
    small_send[:, TOK : 2 * TOK, :] = moved_small(keys[2 * LARGE :])
    values = dot(xmod[...], qkv[2]).astype(BF16)
    small_send[:, 2 * TOK : 3 * TOK, :] = moved_small(values[2 * LARGE :])
    start("small_far")
    for slot, rows in ((1, keys[0:LARGE]), (2, values[0:LARGE]), (3, keys[LARGE : 2 * LARGE]), (4, values[LARGE : 2 * LARGE])):
        large_send[:, slot * TOK : (slot + 1) * TOK, :] = moved_large(rows)
    small_queries = normalize(dot(xmod[2 * LARGE :, :], qkv[0])) * scales
    small_send[:, 0:TOK, :] = moved_small(small_queries.astype(BF16))
    start("small_near")
    small_near[u] = small_send[u]
    large_queries = normalize(dot(xmod[0:LARGE, :], qkv[0])) * scales
    large_send[:, 0:TOK, :] = moved_large(large_queries.astype(BF16))
    start("large_near")
    large_near[u] = large_send[u]
    arrive("ay")
    arrive("bx")
    start("ax")
    start("by")

    lanes = iota((W, W), 1) >> 6
    key = iota((W, W), 0)

    def by_head(rows):
        return [
            jnp.where(lanes[0:LARGE] == k, rows, jnp.zeros_like(rows)) for k in range(4)
        ]

    def offer(index, values, valid):
        for k in range(4):
            row = (index * 4 + k) * W
            use = lanes == k
            if valid is not None:
                use = use & valid
            vext[row : row + W, 0:W] = jnp.where(use, values, jnp.zeros_like(values))
            vext[row : row + W, W : 2 * W] = flags(use)

    def weigh(index, queries, keys):
        for k in range(4):
            column = (index * 4 + k) * W
            weights[:, column : column + W] = jnp.exp(dot_nt(queries[k], keys)).astype(BF16)

    def attend(queries, keys, out):
        for index, block in enumerate(keys):
            weigh(index, queries, block)
        used = len(keys) * 4 * W
        sums = dot(weights[:, 0:used], vext[0:used, :])
        out[...] = (sums[:, 0:W] / sums[:, W : 2 * W]).astype(BF16).reshape(HALF, TOK, W)

    arrive("cache")
    cache_keys = cache_recv[:, 0:16, :].reshape(W, W)
    offer(0, cache_recv[:, 16:32, :].reshape(W, W), key < W - 1)
    arrive("small_near")
    arrive("small_far")
    small_keys = jnp.concatenate(
        [small_near[:, TOK : 2 * TOK, :].reshape(LARGE, W), small_far[:, 0:TOK, :].reshape(LARGE, W)], axis=0
    )
    small_values = jnp.concatenate(
        [small_near[:, 2 * TOK : 3 * TOK, :].reshape(LARGE, W), small_far[:, TOK : 2 * TOK, :].reshape(LARGE, W)],
        axis=0,
    )
    map_row = (key >> 4) + HALF * zh * jnp.where(key < LARGE, 1, -1)
    offer(1, small_values, ((key & 15) < S13) & (map_row < S13))
    attend(by_head(small_near[:, 0:TOK, :].reshape(LARGE, W)), [cache_keys, small_keys], att_small)
    gathers[0].start()

    arrive("large_near")
    large_keys = jnp.concatenate(
        [large_near[:, k * TOK : (k + 1) * TOK, :].reshape(LARGE, W) for k in (1, 3)], axis=0
    )
    large_values = jnp.concatenate(
        [large_near[:, k * TOK : (k + 1) * TOK, :].reshape(LARGE, W) for k in (2, 4)], axis=0
    )
    offer(2, large_values, None)
    attend(
        by_head(large_near[:, 0:TOK, :].reshape(LARGE, W)), [cache_keys, small_keys, large_keys], att_large
    )
    gathers[1].start()
    arrive("ax")
    arrive("by")
    start("wc")

    r, c = iota((PADDED, LARGE), 0), iota((PADDED, LARGE), 1)
    to_row = flags(c == (r & 7) * TOK + (r >> 3))
    kept = seq < S13

    def project_small(side):
        def step(i):
            inner = pl.multiple_of(i * W, W)
            outer = pl.ds(pl.multiple_of(side * SECOND + inner, 128), W)
            branch = dot(small_all[...], wout[side, :, pl.ds(inner, W)])
            gate = mod[2, :, outer]
            for j in range(S13):
                rows = gate * branch[j * IMG : (j + 1) * IMG]
                o13[j, :, outer] = jnp.where(kept, rows, jnp.zeros_like(rows)).astype(BF16)

        over(0, WIDE // W, step)

    def project_large(side):
        def step(i):
            inner = pl.multiple_of(i * W, W)
            outer = pl.ds(pl.multiple_of(side * SECOND + inner, 128), W)
            branch = dot(large_all[...], wout[side, :, pl.ds(inner, W)])
            gate = mod[2, :, outer]
            for b in range(IMG):
                o16[b, :, outer] = (gate[b : b + 1] * branch[b * S16 : (b + 1) * S16]).astype(BF16)

        over(0, WIDE // W, step)

    gathers[0].arrive()
    for k in range(HEADSETS):
        small_all[:, k * W : (k + 1) * W] = dot(to_row, small_recv[k].reshape(LARGE, W)).astype(BF16)
    project_small(core)
    gathers[1].arrive()
    for k in range(HEADSETS):
        large_all[:, k * W : (k + 1) * W] = large_recv[k].reshape(LARGE, W)
    project_large(core)
    arrive("wc")
    both_all[0:PADDED, :] = small_all[...]
    both_all[PADDED:, :] = large_all[...]

    def project_both(i):
        side = 1 - core
        inner = pl.multiple_of(i * W, W)
        outer = pl.ds(pl.multiple_of(side * SECOND + inner, 128), W)
        branch = dot(both_all[...], wout[side, :, pl.ds(inner, W)])
        gate = mod[2, :, outer]
        for j in range(S13):
            rows = gate * branch[j * IMG : (j + 1) * IMG]
            o13[j, :, outer] = jnp.where(kept, rows, jnp.zeros_like(rows)).astype(BF16)
        for b in range(IMG):
            rows = branch[PADDED + b * S16 : PADDED + (b + 1) * S16]
            o16[b, :, outer] = (gate[b : b + 1] * rows).astype(BF16)

    over(0, WIDE // W, project_both)

    for copy in partner:
        copy.wait_send()
    for name in groups:
        sent(name)
    for gather in gathers:
        gather.sent()


def hand_on(a_ref, b_ref, a_out, b_out, sem):
    copies = [
        pltpu.make_async_copy(source.at[i : i + n], target.at[i : i + n], sem.at[k])
        for k, (source, target, i, n) in enumerate(
            ((a_ref, a_out, 0, 7), (a_ref, a_out, 7, 6), (b_ref, b_out, 0, 4), (b_ref, b_out, 4, 4))
        )
    ]
    for copy in copies:
        copy.start()
    for copy in copies:
        copy.wait()


def body(
    map_thirteen, kv_cache, class_labels, class_table, sampled_ids, codebook, feature_sum,
    embed_weight, embed_bias, position_table, qkv_weight, out_weight, head_scale,
):
    owned = class_table.shape[0]
    vocabulary = codebook.shape[0]
    vmem = pl.BlockSpec(memory_space=pltpu.VMEM)
    anywhere = pl.BlockSpec(memory_space=pl.ANY)
    dma = pltpu.SemaphoreType.DMA
    o13, o16 = pl.pallas_call(
        kernel,
        out_shape=(
            jax.ShapeDtypeStruct((S13, IMG, D), BF16),
            jax.ShapeDtypeStruct((IMG, S16, D), BF16),
        ),
        in_specs=[anywhere] * 13,
        out_specs=(vmem, vmem),
        scratch_shapes=[
            pltpu.SMEM((IMG,), jnp.int32),
            pltpu.SMEM(head_scale.shape, F32),
            pltpu.VMEM((S13, IMG, S13), jnp.int32),
            pltpu.VMEM((IMG, 16, 2, W), BF16),
            pltpu.VMEM((IMG, 1, S16 * 32), F32),
            pltpu.VMEM((D,), F32),
            pltpu.VMEM((1, S16, D), BF16),
            pltpu.VMEM((SMALL, D), BF16),
            pltpu.VMEM((3, owned, W), BF16),
            pltpu.VMEM((32, vocabulary), F32),
            pltpu.VMEM((32, D), F32),
            pltpu.VMEM((3, D, W), BF16),
            pltpu.VMEM((2, HEADSETS * W, WIDE), BF16),
            pltpu.VMEM((IMG, 32, W), BF16),
            pltpu.VMEM((16, 32, W), BF16),
            pltpu.VMEM((HEADSETS, 32, W), BF16),
            pltpu.VMEM((HALF, 32, W), BF16),
            pltpu.VMEM((3, IMG, D), F32),
            pltpu.VMEM((DPS, S16, PART), BF16),
            pltpu.VMEM((IMG, 1, S16 * 32), F32),
            pltpu.VMEM((4, S13, IMG, 128), jnp.int32),
            pltpu.VMEM((ROWS, D), F32),
            pltpu.VMEM((ROWS, D), BF16),
            pltpu.VMEM((IMG, 3 * TOK, W), BF16),
            pltpu.VMEM((HALF, 3 * TOK, W), BF16),
            pltpu.VMEM((HALF, 2 * TOK, W), BF16),
            pltpu.VMEM((IMG, 5 * TOK, W), BF16),
            pltpu.VMEM((HALF, 5 * TOK, W), BF16),
            pltpu.VMEM((LARGE, 12 * W), BF16),
            pltpu.VMEM((12 * W, 2 * W), BF16),
            pltpu.VMEM((HALF, TOK, W), BF16),
            pltpu.VMEM((HALF, TOK, W), BF16),
            pltpu.VMEM((HEADSETS, HALF, TOK, W), BF16),
            pltpu.VMEM((HEADSETS, HALF, TOK, W), BF16),
            pltpu.VMEM((PADDED, HEADSETS * W), BF16),
            pltpu.VMEM((LARGE, HEADSETS * W), BF16),
            pltpu.VMEM((PADDED + LARGE, HEADSETS * W), BF16),
            dma((14,)),
        ]
        + [dma((n,)) for n in (
            4, 4, 8, 8, 2, 2, 4, 4, 16, 16, 8, 8, 8, 8, 8, 8, 32, 32, 32, 32, 8, 8, 8, 8, 16, 16, 16, 16, 16, 16, 16, 16, 4, 4
        )],
        compiler_params=pltpu.CompilerParams(
            collective_id=0, has_side_effects=True, vmem_limit_bytes=VMEM_LIMIT
        ),
        cost_estimate=pl.CostEstimate(flops=3_000_000_000, bytes_accessed=12_000_000, transcendentals=1_000_000),
    )(
        class_labels,
        head_scale,
        sampled_ids.transpose(1, 0, 2),
        kv_cache,
        feature_sum,
        embed_bias,
        position_table,
        map_thirteen.reshape(IMG, S13, D).transpose(1, 0, 2).reshape(SMALL, D),
        class_table.transpose(1, 0, 2),
        codebook.T,
        embed_weight,
        qkv_weight.transpose(1, 0, 2),
        out_weight,
    )
    o13, o16 = pl.pallas_call(
        hand_on,
        out_shape=(
            jax.ShapeDtypeStruct((S13, IMG, D), BF16),
            jax.ShapeDtypeStruct((IMG, S16, D), BF16),
        ),
        in_specs=[vmem] * 2,
        out_specs=(anywhere, anywhere),
        scratch_shapes=[dma((4,))],
        cost_estimate=pl.CostEstimate(flops=0, bytes_accessed=1_800_000, transcendentals=0),
    )(o13, o16)
    return o13.transpose(1, 0, 2)[:, None], o16[:, None]


def solution(mesh):
    placed = (
        P("dp", "seq", None, None),
        P("dp", "seq", None, "head"),
        P("dp"),
        P("head", None, None),
        P("dp", None, None),
        P(),
        P("dp", "seq", None),
        P(),
        P(),
        P("seq", None, None),
        P(None, None, "head"),
        P("head", None),
        P("head"),
    )
    return jax.shard_map(
        body,
        mesh=mesh,
        in_specs=placed,
        out_specs=(P("dp", "seq", None, None), P("dp", "seq", None, None)),
        check_vma=False,
    )
```

```python
import functools

import jax
import jax.numpy as jnp
from jax import lax
from jax.experimental import pallas as pl
from jax.experimental.pallas import tpu as pltpu
from jax.sharding import PartitionSpec as P

MESH = pl.DeviceIdType.MESH
S13 = 13
S16 = 16
D = 1920
W = 256
IMG = 8
HALF = 8
HEADSETS = 4
DPS = 4
TOK = 16
LARGE = IMG * S16
SMALL = IMG * S13
PADDED = SMALL + IMG
ROWS = 2 * LARGE + PADDED
SPAN = 512
PART = 512
VIA_X = 768
WIDE = 1024
SECOND = D - WIDE
F32 = jnp.float32
BF16 = jnp.bfloat16
VMEM_LIMIT = 58 * 1024 * 1024


def dot(a, b):
    return jnp.dot(a, b, preferred_element_type=F32)


def dot_nt(a, b):
    return lax.dot_general(a, b, (((1,), (1,)), ((), ())), preferred_element_type=F32)


def iota(shape, axis):
    return lax.broadcasted_iota(jnp.int32, shape, axis)


def flags(condition):
    return jnp.where(condition, 1.0, 0.0).astype(BF16)


def split(x):
    high = x.astype(BF16)
    return high, (x - high.astype(F32)).astype(BF16)


def layer_norm(x):
    centred = x - jnp.mean(x, axis=-1, keepdims=True)
    variance = jnp.mean(centred * centred, axis=-1, keepdims=True)
    return centred * lax.rsqrt(variance + 1e-06)


def remote(src, dst, send, recv, **device):
    return pltpu.make_async_remote_copy(
        src_ref=src, dst_ref=dst, send_sem=send, recv_sem=recv, device_id=device, device_id_type=MESH
    )


def kernel(
    labels_hbm, scale_hbm, ids_hbm, cache_hbm, features_hbm, bias_hbm, position_hbm,
    thirteen_hbm, table_hbm, codebook_hbm, embed_hbm, qkv_hbm, out_hbm,
    o13_hbm, o16_hbm,
    o13, o16, labels, head_scale, ids, cache, feature_sum, bias, position,
    thirteen, table, codebook, embed, qkv, wout,
    cache_send, cache_recv, mod_a, mod_b, mod, far_position, far_features, id_lanes, xhat, xmod,
    small_send, small_near, small_far, large_send, large_near,
    weights, vext, att_small, att_large, small_recv, large_recv, small_all, large_all, both_all,
    local_sem,
    ma_s, ma_r, mb_s, mb_r, fp_s, fp_r, sp_s, sp_r, ca_s, ca_r, sn_s, sn_r, sf_s, sf_r, ln_s, ln_r,
    as_s, as_r, al_s, al_r, fs_s, fl_s,
    wz_s, wz_r, ay_s, ay_r, bx_s, bx_r, ax_s, ax_r, by_s, by_r, wc_s, wc_r,
):
    x = lax.axis_index("dp")
    seq = lax.axis_index("seq")
    h = lax.axis_index("head")
    zh, u = seq // HALF, seq % HALF
    y, core = u // 2, u % 2
    me = h * HALF + u

    def in_half(place):
        return zh * HALF + place

    def in_other(place):
        return (1 - zh) * HALF + place

    barrier = pltpu.get_barrier_semaphore()

    def greet_half(d, c):
        p = (me + d) % (HEADSETS * HALF)
        pl.semaphore_signal(
            barrier, inc=1, device_id={"seq": in_half(p % HALF), "head": p // HALF}, device_id_type=MESH
        )
        return c

    def greet_other(d, c):
        pl.semaphore_signal(
            barrier, inc=1, device_id={"seq": in_other((u + d) % HALF)}, device_id_type=MESH
        )
        return c

    def greet_dp(d, c):
        pl.semaphore_signal(barrier, inc=1, device_id={"dp": (x + d) % DPS}, device_id_type=MESH)
        return c

    lax.fori_loop(0, HALF, greet_other, 0)
    lax.fori_loop(1, HEADSETS * HALF, greet_half, 0)
    lax.fori_loop(1, DPS, greet_dp, 0)

    col0 = pl.multiple_of(u * W - (u // 7) * 128, 128)
    loads = [
        (labels_hbm, labels),
        (table_hbm.at[:, :, pl.ds(col0, W)], table),
        (cache_hbm, cache),
        (position_hbm, position),
        (features_hbm, feature_sum),
        (ids_hbm, ids),
        (codebook_hbm, codebook),
        (out_hbm.at[:, pl.ds(0, WIDE)], wout.at[0, pl.ds(pl.multiple_of(h * W, W), W), :]),
        (out_hbm.at[:, pl.ds(SECOND, WIDE)], wout.at[1, pl.ds(pl.multiple_of(h * W, W), W), :]),
        (thirteen_hbm, thirteen),
        (embed_hbm, embed),
        (bias_hbm, bias),
        (scale_hbm, head_scale),
        (qkv_hbm, qkv),
    ]
    names = (
        "labels", "table", "cache", "position", "features", "ids", "codebook", "out0", "out1", "thirteen",
        "embed", "bias", "scale", "qkv",
    )
    loads = {
        name: pltpu.make_async_copy(a, b, local_sem.at[i]) for i, (name, (a, b)) in enumerate(zip(names, loads))
    }
    for load in loads.values():
        load.start()

    def mod_a_copy(d):
        to = (h + d) % HEADSETS
        return remote(mod_a.at[h], mod_a.at[h], ma_s.at[to], ma_r.at[h], head=to)

    def mod_b_copy(d):
        to = (u + d) % HALF
        return remote(mod_b.at[u], mod_b.at[u], mb_s.at[to], mb_r.at[u], seq=in_half(to))

    def spread_copy(d):
        to = (x + d) % DPS
        return remote(far_position.at[x], far_position.at[x], sp_s.at[to], sp_r.at[x], dp=to)

    def cache_copy(d):
        to = (seq + d) % 16
        return remote(cache_send.at[to % HALF], cache_recv.at[seq], ca_s.at[to], ca_r.at[seq], seq=to)

    def small_near_copy(d):
        to = (u + d) % HALF
        return remote(small_send.at[to], small_near.at[u], sn_s.at[to], sn_r.at[u], seq=in_half(to))

    def small_far_copy(d):
        to = (u + d) % HALF
        return remote(
            small_send.at[to, pl.ds(TOK, 2 * TOK), :], small_far.at[u], sf_s.at[to], sf_r.at[u],
            seq=in_other(to),
        )

    def large_near_copy(d):
        to = (u + d) % HALF
        return remote(large_send.at[to], large_near.at[u], ln_s.at[to], ln_r.at[u], seq=in_half(to))

    def peer(d):
        return (me + d) % (HEADSETS * HALF)

    relay = (h % 3) > 0
    relayed, beyond = 3 * (2 - h), 3 * (h - 1)

    class Gather:
        def __init__(self, source, target, send, recv, forward):
            self.source, self.target, self.send, self.recv, self.forward = source, target, send, recv, forward

        def copy(self, p):
            return remote(
                self.source.at[p % HALF], self.target.at[h, u], self.send.at[p], self.recv.at[me],
                seq=in_half(p % HALF), head=p // HALF,
            )

        def direct(self, action):
            def step(d):
                p = peer(d)

                getattr(self.copy(p), action)()

            over(1, HEADSETS * HALF, step)

        def start(self):
            self.direct("start")
            self.target[h, u] = self.source[u]

        def slot(self, part, b):
            return self.target.at[part, b], self.recv.at[part * HALF + b]

        def passing(self, b):
            ref, sem = self.slot(relayed, b)
            return remote(ref, ref, self.forward.at[b], sem, head=beyond)

        def pass_on(self):
            @pl.when(relay)
            def _():
                def step(d):
                    b = (u + d) % HALF
                    landed(self.slot(relayed, b))
                    self.passing(b).start()

                over(0, HALF, step)

        def arrive(self):
            def step(d):
                p = peer(d)

                landed(self.slot(p // HALF, p % HALF))

            over(1, HEADSETS * HALF, step)

        def sent(self):
            self.direct("wait_send")

    gathers = [
        Gather(att_small, small_recv, as_s, as_r, fs_s),
        Gather(att_large, large_recv, al_s, al_r, fl_s),
    ]

    def piece(part, column, start, count):
        rows = pl.ds(pl.multiple_of(part * W + start, 16), count)
        return wout.at[core, rows, 0:VIA_X] if column == 0 else wout.at[core, rows, VIA_X:WIDE]

    def first_rows(column):
        return x * 64 + y * 16 if column == 0 else y * 64 + x * 16

    def wz_copy(i):
        to = (h + 1 + i) % HEADSETS
        ref = piece(h, 0, first_rows(0), 16)
        return remote(ref, ref, wz_s.at[to], wz_r.at[h], head=to)

    def vz_copy(i):
        to = (h + 1 + i) % HEADSETS
        ref = piece(h, 1, first_rows(1), 16)
        return remote(ref, ref, wz_s.at[4 + to], wz_r.at[4 + h], head=to)

    def y_place(i):
        return (y + 1 + i // 3) % 4, (h + 1 + i % 3) % HEADSETS

    def x_place(i):
        return (x + 1 + i // 3) % DPS, (h + 1 + i % 3) % HEADSETS

    def ay_copy(i):
        to, part = y_place(i)
        ref = piece(part, 0, first_rows(0), 16)
        return remote(
            ref, ref, ay_s.at[to * 4 + part], ay_r.at[y * 4 + part], seq=in_half(to * 2 + core)
        )

    def bx_copy(i):
        to, part = x_place(i)
        ref = piece(part, 1, first_rows(1), 16)
        return remote(ref, ref, bx_s.at[to * 4 + part], bx_r.at[x * 4 + part], dp=to)

    def ax_copy(i):
        to, part = x_place(i)
        ref = piece(part, 0, x * 64, 64)
        return remote(ref, ref, ax_s.at[to * 4 + part], ax_r.at[x * 4 + part], dp=to)

    def by_copy(i):
        to, part = y_place(i)
        ref = piece(part, 1, y * 64, 64)
        return remote(
            ref, ref, by_s.at[to * 4 + part], by_r.at[y * 4 + part], seq=in_half(to * 2 + core)
        )

    def wc_copy(i):
        part = (h + 1 + i) % HEADSETS
        ref = wout.at[core, pl.ds(pl.multiple_of(part * W, W), W), :]
        return remote(ref, ref, wc_s.at[part], wc_r.at[part], seq=in_half(u + 1 - 2 * core))

    groups = {
        "mod_a": (1, HEADSETS, mod_a_copy, lambda d: (mod_a.at[(h + d) % HEADSETS], ma_r.at[(h + d) % HEADSETS])),
        "mod_b": (1, HALF, mod_b_copy, lambda d: (mod_b.at[(u + d) % HALF], mb_r.at[(u + d) % HALF])),
        "spread": (1, DPS, spread_copy, lambda d: (far_position.at[(x + d) % DPS], sp_r.at[(x + d) % DPS])),
        "cache": (1, 16, cache_copy, lambda d: (cache_recv.at[(seq + d) % 16], ca_r.at[(seq + d) % 16])),
        "small_near": (
            1, HALF, small_near_copy, lambda d: (small_near.at[(u + d) % HALF], sn_r.at[(u + d) % HALF]),
        ),
        "small_far": (
            0, HALF, small_far_copy, lambda d: (small_far.at[(u + d) % HALF], sf_r.at[(u + d) % HALF]),
        ),
        "large_near": (
            1, HALF, large_near_copy, lambda d: (large_near.at[(u + d) % HALF], ln_r.at[(u + d) % HALF]),
        ),
        "wz": (
            0, 3, wz_copy,
            lambda i: (piece((h + 1 + i) % HEADSETS, 0, first_rows(0), 16), wz_r.at[(h + 1 + i) % HEADSETS]),
        ),
        "vz": (
            0, 3, vz_copy,
            lambda i: (piece((h + 1 + i) % HEADSETS, 1, first_rows(1), 16), wz_r.at[4 + (h + 1 + i) % HEADSETS]),
        ),
        "ay": (
            0, 9, ay_copy,
            lambda i: (
                piece(y_place(i)[1], 0, x * 64 + y_place(i)[0] * 16, 16),
                ay_r.at[y_place(i)[0] * 4 + y_place(i)[1]],
            ),
        ),
        "bx": (
            0, 9, bx_copy,
            lambda i: (
                piece(x_place(i)[1], 1, y * 64 + x_place(i)[0] * 16, 16),
                bx_r.at[x_place(i)[0] * 4 + x_place(i)[1]],
            ),
        ),
        "ax": (
            0, 9, ax_copy,
            lambda i: (
                piece(x_place(i)[1], 0, x_place(i)[0] * 64, 64), ax_r.at[x_place(i)[0] * 4 + x_place(i)[1]],
            ),
        ),
        "by": (
            0, 9, by_copy,
            lambda i: (
                piece(y_place(i)[1], 1, y_place(i)[0] * 64, 64), by_r.at[y_place(i)[0] * 4 + y_place(i)[1]],
            ),
        ),
        "wc": (
            0, 3, wc_copy,
            lambda i: (
                wout.at[1 - core, pl.ds(pl.multiple_of(((h + 1 + i) % HEADSETS) * W, W), W), :],
                wc_r.at[(h + 1 + i) % HEADSETS],
            ),
        ),
    }

    def over(low, high, action):
        def step(d, c):
            action(d)
            return c

        lax.fori_loop(low, high, step, 0)

    def landed(place):
        slot, sem = place
        remote(slot, slot, ma_s.at[0], sem, head=(h + 1) % HEADSETS).wait_recv()

    def start(name):
        low, high, copy, _ = groups[name]
        over(low, high, lambda d: copy(d).start())

    def arrive(name):
        low, high, _, arrival = groups[name]
        over(low, high, lambda d: landed(arrival(d)))

    def sent(name):
        low, high, copy, _ = groups[name]
        over(low, high, lambda d: copy(d).wait_send())

    partner = [
        remote(
            position.at[0, :, pl.ds(pl.multiple_of(x * PART - (x // 3) * 128, 128), PART)], far_position.at[x],
            fp_s.at[0], fp_r.at[0], seq=in_other(u),
        ),
        remote(feature_sum, far_features, fp_s.at[1], fp_r.at[1], seq=in_other(u)),
    ]

    loads["labels"].wait()
    loads["table"].wait()
    owned = table.shape[1]
    rows8 = iota((IMG, owned), 0)
    wanted = jnp.zeros((IMG, owned), jnp.int32)
    for b in range(IMG):
        wanted = jnp.where(rows8 == b, labels[b] - h * owned, wanted)
    onehot = flags(wanted == iota((IMG, owned), 1))
    parts = [dot(onehot, table[t]) for t in range(3)] + [jnp.zeros((IMG, W), F32)]
    mod_a[h] = jnp.concatenate(parts, axis=0).astype(BF16)

    group = flags((iota((W, W), 0) >> 6) == (iota((W, W), 1) >> 6))

    def normalize(v):
        high, low = split(v * v)
        return v * lax.rsqrt(dot(high, group) + dot(low, group) + 1e-06)

    loads["cache"].wait()
    r, c = iota((W, W), 0), iota((W, W), 1)
    to_kind = flags(c == ((r >> 5) * 32 + (r & 15) * 2 + ((r >> 4) & 1)))
    moved = dot(to_kind, cache[...].reshape(W, W))
    moved = jnp.where(((r >> 4) & 1) == 0, normalize(moved), moved)
    cache_send[...] = moved.astype(BF16).reshape(IMG, 32, W)
    cache_recv[seq] = cache_send[u]
    loads["position"].wait()
    loads["features"].wait()
    loads["ids"].wait()

    pl.semaphore_wait(barrier, HEADSETS * HALF - 1 + HALF + DPS - 1)
    start("mod_a")
    loads["out0"].wait()
    loads["out1"].wait()
    start("wz")
    start("vz")
    for copy in partner:
        copy.start()

    taps = []
    for n, row in enumerate((seq, (seq + HALF) % 16)):
        place = 26 * row - 3 + 3 * ((16 - row) // 16)
        lower = place // 32
        upper = lower + 1 - lower // (S13 - 1)
        taps.append((place % 32).astype(F32) * (1.0 / 32.0))
        for t, source in enumerate((ids[lower], ids[upper])):
            for j in range(S13):
                id_lanes[2 * n + t, j] = jnp.broadcast_to(source[:, j : j + 1], (IMG, 128))
    loads["codebook"].wait()

    def look(c, total):
        start_at = pl.multiple_of(c * SPAN, SPAN)
        columns = []
        for q in range(SPAN // 128):
            entry = iota((IMG, 128), 1) + (c * SPAN + q * 128)
            hits = []
            for n in range(2):
                for j in range(S13):
                    hits.append(
                        jnp.where(id_lanes[2 * n, j] == entry, 1.0 - taps[n], 0.0)
                        + jnp.where(id_lanes[2 * n + 1, j] == entry, taps[n], 0.0)
                    )
            columns.append(jnp.concatenate(hits, axis=0).astype(BF16))
        both = jnp.concatenate(split(codebook[:, pl.ds(start_at, SPAN)]), axis=0)
        return total + dot_nt(jnp.concatenate(columns, axis=1), both)

    looked = lax.fori_loop(0, codebook.shape[1] // SPAN, look, jnp.zeros((2 * SMALL, 64), F32))
    looked = looked[:, 0:32] + looked[:, 32:64]

    arrive("mod_a")
    total = mod_a[0].astype(F32)
    for part in range(1, HEADSETS):
        total = total + mod_a[part].astype(F32)
    mod_b[u] = total.astype(BF16)
    start("mod_b")
    start("cache")

    loads["thirteen"].wait()
    first = 2 * LARGE
    for i in range(SMALL // 16):
        xhat[first + 16 * i : first + 16 * i + 16, :] = layer_norm(thirteen[16 * i : 16 * i + 16, :].astype(F32))
    xhat[ROWS - 16 : ROWS - 8, :] = layer_norm(thirteen[SMALL - 8 : SMALL, :].astype(F32))
    xhat[ROWS - 8 : ROWS, :] = jnp.zeros((8, D), F32)
    loads["embed"].wait()
    loads["bias"].wait()
    embed_high, embed_low = split(embed[...])
    embed_parts = jnp.concatenate([embed_high, embed_low, embed_high], axis=0)
    bias_row = bias[...].reshape(1, D)

    def embedded(first, source, rows, table_rows):
        features = []
        for s in range(S16):
            at = max(26 * s - 3, 0)
            low = at // 32
            up = min(low + 1, S13 - 1)
            frac = (at % 32) / 32.0
            features.append(
                source[:, s * 32 : (s + 1) * 32]
                + rows[low * IMG : (low + 1) * IMG] * (1.0 - frac)
                + rows[up * IMG : (up + 1) * IMG] * frac
            )
        high, low = split(jnp.concatenate(features, axis=0))
        xhat[first : first + LARGE, :] = dot(jnp.concatenate([high, high, low], axis=1), embed_parts)
        for i in range(S16 // 2):
            pair = table_rows[2 * i : 2 * i + 2, :].astype(F32)
            pair = jnp.concatenate([jnp.broadcast_to(pair[k : k + 1], (IMG, D)) for k in range(2)], axis=0)
            at = first + 16 * i
            row = xhat[at : at + 16, :] + bias_row + pair
            xhat[at : at + 16, :] = layer_norm(row.astype(BF16).astype(F32))

    partner[0].wait_recv()
    start("spread")
    embedded(0, feature_sum[:, 0, :], looked[0:SMALL], position[0])
    arrive("spread")
    partner[1].wait_recv()
    far_rows = [far_position[k] for k in range(DPS)]
    far_rows[DPS - 1] = far_rows[DPS - 1][:, DPS * PART - D :]
    embedded(LARGE, far_features[:, 0, :], looked[SMALL : 2 * SMALL], jnp.concatenate(far_rows, axis=1))

    arrive("wz")
    arrive("vz")
    start("ay")
    start("bx")
    arrive("mod_b")
    for c in range(HALF):
        chunk = mod_b[c].astype(F32)
        if c == HALF - 1:
            chunk = chunk[:, 128:]
        width = chunk.shape[1]
        mod[0, :, c * W : c * W + width] = chunk[0:8]
        mod[1, :, c * W : c * W + width] = 1.0 + chunk[8:16]
        mod[2, :, c * W : c * W + width] = chunk[16:24]

    def modulate(i):
        at = pl.multiple_of(i * 16, 16)
        rows = xhat[pl.ds(at, 16), :].reshape(2, IMG, D)
        rows = rows * mod[1][None] + mod[0][None]
        xmod[pl.ds(at, 16), :] = rows.reshape(16, D).astype(BF16)

    loads["scale"].wait()
    lane_head = iota((1, W), 1) >> 6
    scales = jnp.zeros((1, W), F32)
    for k in range(4):
        scales = jnp.where(lane_head == k, head_scale[k], scales)

    over(0, ROWS // 16, modulate)
    loads["qkv"].wait()
    r, c = iota((LARGE, PADDED), 0), iota((LARGE, PADDED), 1)
    small_to_image = flags(((r & 15) < S13) & (c == (r & 15) * IMG + (r >> 4)))
    r, c = iota((LARGE, LARGE), 0), iota((LARGE, LARGE), 1)
    large_to_image = flags(c == (r & 15) * IMG + (r >> 4))

    def moved_small(rows):
        return dot(small_to_image, rows).astype(BF16).reshape(IMG, TOK, W)

    def moved_large(rows):
        return dot(large_to_image, rows).astype(BF16).reshape(IMG, TOK, W)

    keys = normalize(dot(xmod[...], qkv[1])).astype(BF16)
    small_send[:, TOK : 2 * TOK, :] = moved_small(keys[2 * LARGE :])
    values = dot(xmod[...], qkv[2]).astype(BF16)
    small_send[:, 2 * TOK : 3 * TOK, :] = moved_small(values[2 * LARGE :])
    start("small_far")
    for slot, rows in ((1, keys[0:LARGE]), (2, values[0:LARGE]), (3, keys[LARGE : 2 * LARGE]), (4, values[LARGE : 2 * LARGE])):
        large_send[:, slot * TOK : (slot + 1) * TOK, :] = moved_large(rows)
    small_queries = normalize(dot(xmod[2 * LARGE :, :], qkv[0])) * scales
    small_send[:, 0:TOK, :] = moved_small(small_queries.astype(BF16))
    start("small_near")
    small_near[u] = small_send[u]
    large_queries = normalize(dot(xmod[0:LARGE, :], qkv[0])) * scales
    large_send[:, 0:TOK, :] = moved_large(large_queries.astype(BF16))
    start("large_near")
    large_near[u] = large_send[u]
    arrive("ay")
    arrive("bx")
    start("ax")
    start("by")

    lanes = iota((W, W), 1) >> 6
    key = iota((W, W), 0)

    def by_head(rows):
        return [
            jnp.where(lanes[0:LARGE] == k, rows, jnp.zeros_like(rows)) for k in range(4)
        ]

    def offer(index, values, valid):
        for k in range(4):
            row = (index * 4 + k) * W
            use = lanes == k
            if valid is not None:
                use = use & valid
            vext[row : row + W, 0:W] = jnp.where(use, values, jnp.zeros_like(values))
            vext[row : row + W, W : 2 * W] = flags(use)

    def weigh(index, queries, keys):
        for k in range(4):
            column = (index * 4 + k) * W
            weights[:, column : column + W] = jnp.exp(dot_nt(queries[k], keys)).astype(BF16)

    def attend(queries, keys, out):
        for index, block in enumerate(keys):
            weigh(index, queries, block)
        used = len(keys) * 4 * W
        sums = dot(weights[:, 0:used], vext[0:used, :])
        out[...] = (sums[:, 0:W] / sums[:, W : 2 * W]).astype(BF16).reshape(HALF, TOK, W)

    arrive("cache")
    cache_keys = cache_recv[:, 0:16, :].reshape(W, W)
    offer(0, cache_recv[:, 16:32, :].reshape(W, W), key < W - 1)
    arrive("small_near")
    arrive("small_far")
    small_keys = jnp.concatenate(
        [small_near[:, TOK : 2 * TOK, :].reshape(LARGE, W), small_far[:, 0:TOK, :].reshape(LARGE, W)], axis=0
    )
    small_values = jnp.concatenate(
        [small_near[:, 2 * TOK : 3 * TOK, :].reshape(LARGE, W), small_far[:, TOK : 2 * TOK, :].reshape(LARGE, W)],
        axis=0,
    )
    map_row = (key >> 4) + HALF * zh * jnp.where(key < LARGE, 1, -1)
    offer(1, small_values, ((key & 15) < S13) & (map_row < S13))
    attend(by_head(small_near[:, 0:TOK, :].reshape(LARGE, W)), [cache_keys, small_keys], att_small)
    gathers[0].start()

    arrive("large_near")
    large_keys = jnp.concatenate(
        [large_near[:, k * TOK : (k + 1) * TOK, :].reshape(LARGE, W) for k in (1, 3)], axis=0
    )
    large_values = jnp.concatenate(
        [large_near[:, k * TOK : (k + 1) * TOK, :].reshape(LARGE, W) for k in (2, 4)], axis=0
    )
    offer(2, large_values, None)
    attend(
        by_head(large_near[:, 0:TOK, :].reshape(LARGE, W)), [cache_keys, small_keys, large_keys], att_large
    )
    gathers[1].start()
    arrive("ax")
    arrive("by")
    start("wc")

    r, c = iota((PADDED, LARGE), 0), iota((PADDED, LARGE), 1)
    to_row = flags(c == (r & 7) * TOK + (r >> 3))
    kept = seq < S13

    def project_small(side):
        def step(i):
            inner = pl.multiple_of(i * W, W)
            outer = pl.ds(pl.multiple_of(side * SECOND + inner, 128), W)
            branch = dot(small_all[...], wout[side, :, pl.ds(inner, W)])
            gate = mod[2, :, outer]
            for j in range(S13):
                rows = gate * branch[j * IMG : (j + 1) * IMG]
                o13[j, :, outer] = jnp.where(kept, rows, jnp.zeros_like(rows)).astype(BF16)

        over(0, WIDE // W, step)

    def project_large(side):
        def step(i):
            inner = pl.multiple_of(i * W, W)
            outer = pl.ds(pl.multiple_of(side * SECOND + inner, 128), W)
            branch = dot(large_all[...], wout[side, :, pl.ds(inner, W)])
            gate = mod[2, :, outer]
            for b in range(IMG):
                o16[b, :, outer] = (gate[b : b + 1] * branch[b * S16 : (b + 1) * S16]).astype(BF16)

        over(0, WIDE // W, step)

    def written(first, width, sem):
        where = pl.ds(pl.multiple_of(first, 128), width)
        return [
            pltpu.make_async_copy(o13.at[:, :, where], o13_hbm.at[:, :, where], local_sem.at[sem]),
            pltpu.make_async_copy(o16.at[:, :, where], o16_hbm.at[:, :, where], local_sem.at[sem + 1]),
        ]

    gathers[0].arrive()
    for k in range(HEADSETS):
        small_all[:, k * W : (k + 1) * W] = dot(to_row, small_recv[k].reshape(LARGE, W)).astype(BF16)
    project_small(core)
    gathers[1].arrive()
    for k in range(HEADSETS):
        large_all[:, k * W : (k + 1) * W] = large_recv[k].reshape(LARGE, W)
    project_large(core)
    write_own = written(core * SECOND, WIDE, 14)
    for copy in write_own:
        copy.start()
    arrive("wc")
    both_all[0:PADDED, :] = small_all[...]
    both_all[PADDED:, :] = large_all[...]

    def project_both(first, width):
        side = 1 - core
        inner = pl.multiple_of((1 - core) * (WIDE - SECOND) + first, 128)
        outer = pl.ds(pl.multiple_of(side * SECOND + inner, 128), width)
        branch = dot(both_all[...], wout[side, :, pl.ds(inner, width)])
        gate = mod[2, :, outer]
        for j in range(S13):
            rows = gate * branch[j * IMG : (j + 1) * IMG]
            o13[j, :, outer] = jnp.where(kept, rows, jnp.zeros_like(rows)).astype(BF16)
        for b in range(IMG):
            rows = branch[PADDED + b * S16 : PADDED + (b + 1) * S16]
            o16[b, :, outer] = (gate[b : b + 1] * rows).astype(BF16)

    over(0, SECOND // W, lambda i: project_both(i * W, W))
    project_both(SECOND // W * W, SECOND % W)
    write_other = written((1 - core) * WIDE, SECOND, 16)
    for copy in write_other:
        copy.start()

    for copy in partner:
        copy.wait_send()
    for name in groups:
        sent(name)
    for gather in gathers:
        gather.sent()
    for copy in write_own + write_other:
        copy.wait()


def hand_on(a_ref, b_ref, a_out, b_out, sem):
    copies = [
        pltpu.make_async_copy(source.at[i : i + n], target.at[i : i + n], sem.at[k])
        for k, (source, target, i, n) in enumerate(
            ((a_ref, a_out, 0, 7), (a_ref, a_out, 7, 6), (b_ref, b_out, 0, 4), (b_ref, b_out, 4, 4))
        )
    ]
    for copy in copies:
        copy.start()
    for copy in copies:
        copy.wait()


def body(
    map_thirteen, kv_cache, class_labels, class_table, sampled_ids, codebook, feature_sum,
    embed_weight, embed_bias, position_table, qkv_weight, out_weight, head_scale,
):
    owned = class_table.shape[0]
    vocabulary = codebook.shape[0]
    vmem = pl.BlockSpec(memory_space=pltpu.VMEM)
    anywhere = pl.BlockSpec(memory_space=pl.ANY)
    dma = pltpu.SemaphoreType.DMA
    o13, o16 = pl.pallas_call(
        kernel,
        out_shape=(
            jax.ShapeDtypeStruct((S13, IMG, D), BF16),
            jax.ShapeDtypeStruct((IMG, S16, D), BF16),
        ),
        in_specs=[anywhere] * 13,
        out_specs=(anywhere, anywhere),
        scratch_shapes=[
            pltpu.VMEM((S13, IMG, D), BF16),
            pltpu.VMEM((IMG, S16, D), BF16),
            pltpu.SMEM((IMG,), jnp.int32),
            pltpu.SMEM(head_scale.shape, F32),
            pltpu.VMEM((S13, IMG, S13), jnp.int32),
            pltpu.VMEM((IMG, 16, 2, W), BF16),
            pltpu.VMEM((IMG, 1, S16 * 32), F32),
            pltpu.VMEM((D,), F32),
            pltpu.VMEM((1, S16, D), BF16),
            pltpu.VMEM((SMALL, D), BF16),
            pltpu.VMEM((3, owned, W), BF16),
            pltpu.VMEM((32, vocabulary), F32),
            pltpu.VMEM((32, D), F32),
            pltpu.VMEM((3, D, W), BF16),
            pltpu.VMEM((2, HEADSETS * W, WIDE), BF16),
            pltpu.VMEM((IMG, 32, W), BF16),
            pltpu.VMEM((16, 32, W), BF16),
            pltpu.VMEM((HEADSETS, 32, W), BF16),
            pltpu.VMEM((HALF, 32, W), BF16),
            pltpu.VMEM((3, IMG, D), F32),
            pltpu.VMEM((DPS, S16, PART), BF16),
            pltpu.VMEM((IMG, 1, S16 * 32), F32),
            pltpu.VMEM((4, S13, IMG, 128), jnp.int32),
            pltpu.VMEM((ROWS, D), F32),
            pltpu.VMEM((ROWS, D), BF16),
            pltpu.VMEM((IMG, 3 * TOK, W), BF16),
            pltpu.VMEM((HALF, 3 * TOK, W), BF16),
            pltpu.VMEM((HALF, 2 * TOK, W), BF16),
            pltpu.VMEM((IMG, 5 * TOK, W), BF16),
            pltpu.VMEM((HALF, 5 * TOK, W), BF16),
            pltpu.VMEM((LARGE, 12 * W), BF16),
            pltpu.VMEM((12 * W, 2 * W), BF16),
            pltpu.VMEM((HALF, TOK, W), BF16),
            pltpu.VMEM((HALF, TOK, W), BF16),
            pltpu.VMEM((HEADSETS, HALF, TOK, W), BF16),
            pltpu.VMEM((HEADSETS, HALF, TOK, W), BF16),
            pltpu.VMEM((PADDED, HEADSETS * W), BF16),
            pltpu.VMEM((LARGE, HEADSETS * W), BF16),
            pltpu.VMEM((PADDED + LARGE, HEADSETS * W), BF16),
            dma((18,)),
        ]
        + [dma((n,)) for n in (
            4, 4, 8, 8, 2, 2, 4, 4, 16, 16, 8, 8, 8, 8, 8, 8, 32, 32, 32, 32, 8, 8, 8, 8, 16, 16, 16, 16, 16, 16, 16, 16, 4, 4
        )],
        compiler_params=pltpu.CompilerParams(
            collective_id=0, has_side_effects=True, vmem_limit_bytes=VMEM_LIMIT
        ),
        cost_estimate=pl.CostEstimate(flops=3_000_000_000, bytes_accessed=12_000_000, transcendentals=1_000_000),
    )(
        class_labels,
        head_scale,
        sampled_ids.transpose(1, 0, 2),
        kv_cache,
        feature_sum,
        embed_bias,
        position_table,
        map_thirteen.reshape(IMG, S13, D).transpose(1, 0, 2).reshape(SMALL, D),
        class_table.transpose(1, 0, 2),
        codebook.T,
        embed_weight,
        qkv_weight.transpose(1, 0, 2),
        out_weight,
    )
    o13, o16 = pl.pallas_call(
        hand_on,
        out_shape=(
            jax.ShapeDtypeStruct((S13, IMG, D), BF16),
            jax.ShapeDtypeStruct((IMG, S16, D), BF16),
        ),
        in_specs=[vmem] * 2,
        out_specs=(anywhere, anywhere),
        scratch_shapes=[dma((4,))],
        cost_estimate=pl.CostEstimate(flops=0, bytes_accessed=1_800_000, transcendentals=0),
    )(o13, o16)
    return o13.transpose(1, 0, 2)[:, None], o16[:, None]


def solution(mesh):
    placed = (
        P("dp", "seq", None, None),
        P("dp", "seq", None, "head"),
        P("dp"),
        P("head", None, None),
        P("dp", None, None),
        P(),
        P("dp", "seq", None),
        P(),
        P(),
        P("seq", None, None),
        P(None, None, "head"),
        P("head", None),
        P("head"),
    )
    return jax.shard_map(
        body,
        mesh=mesh,
        in_specs=placed,
        out_specs=(P("dp", "seq", None, None), P("dp", "seq", None, None)),
        check_vma=False,
    )
```
